128 devices in a mesh: blk: 16 (over y, x_hi, core), uly: 8 (over x_lo, z).
Axes of the slice: x: 4 (x_hi: 2, x_lo: 2; x = x_hi * 2 + x_lo), y: 4, z: 4, core: 2. Of those that a mesh axis runs over, the one named last changes fastest.
Arguments:
- queries: bfloat16 [16384, 12288], P(('blk', 'uly')), may hold values from -16 to 16
- latents: bfloat16 [16384, 576], P(('blk', 'uly')), may hold values from -16 to 16
- block_mask: int32 [128, 128], replicated, may hold values from 0 to 1, as said below
- w_key: bfloat16 [512, 8192], P(None, 'uly'), may hold values from -0.25 to 0.25
- w_value: bfloat16 [512, 8192], P(None, 'uly'), may hold values from -0.25 to 0.25
- w_out: bfloat16 [8192, 3584], P('uly'), may hold values from -0.0625 to 0.0625
Outputs:
- mixed: bfloat16 [16384, 3584], P(('blk', 'uly'))
The draws below stay inside these ranges and needn't reach their ends.
Inputs may be any that keep to these rules, and one draw needn't show every extreme that they name: block_mask[i, j] is 1 exactly when block j is block i itself or an ancestor of block i in a tree rooted at block 0 in which every block's parent comes before it; no block has more than 8 such blocks, and some block has exactly 8.
All inputs are finite; a program needn't handle non-finite values.
Results may differ from the reference program's by a relative error of at most 0.02.
Values may be sent and summed in bfloat16 or wider, within the bound.
No kernel may reach another device: no remote copies, remote signals or barrier semaphores. Data moves between devices by JAX's collectives and lax.ppermute only.
A program may use at most 192 MiB of HBM per device.

```python
import math
import jax
import jax.numpy as jnp
from jax import lax

BLOCK = 128
DEPTH = 8
HEADS = 64
NOPE = 128
ROPE = 64
VDIM = 128
LATENT = 512
OUT_COLS = 3584
TOKENS = 16384


def draw_queries(key, part):
    key = jax.random.fold_in(key, 9)
    base_draw = jax.random.truncated_normal(key, -6.0, 6.0, (TOKENS, HEADS * (NOPE + ROPE)), jnp.float32)
    return base_draw.astype(jnp.bfloat16)


def draw_latents(key, part):
    key = jax.random.fold_in(key, 5)
    base_draw = jax.random.truncated_normal(key, -6.0, 6.0, (TOKENS, LATENT + ROPE), jnp.float32)
    return base_draw.astype(jnp.bfloat16)


def draw_block_mask(key, part):
    key = jax.random.fold_in(key, 13)
    blocks_all = TOKENS // BLOCK
    coin_key, pick_key = jax.random.split(key)
    coin_draws = jax.random.randint(coin_key, (blocks_all,), 0, 4)
    pick_draws = jax.random.randint(pick_key, (blocks_all,), 0, 1 << 30)
    indices = jnp.arange(blocks_all, dtype=jnp.int32)

    def place_block(depths, inputs):
        block_id, coin_value, pick_value = inputs
        previous = jnp.maximum(block_id - 1, 0)
        candidate = pick_value % jnp.maximum(block_id, 1)
        forked = jnp.where(depths[candidate] < DEPTH, candidate, 0)
        extend = (block_id < DEPTH) | (coin_value > 0) & (depths[previous] < DEPTH)
        parent = jnp.where(extend, previous, forked)
        level_here = jnp.where(block_id == 0, 1, depths[parent] + 1)
        parent = jnp.where(block_id == 0, -1, parent)
        return (depths.at[block_id].set(level_here), parent)
    start_depths = jnp.zeros((blocks_all,), jnp.int32)
    unused_depths, parents = lax.scan(place_block, start_depths, (indices, coin_draws, pick_draws))
    linked = (parents[:, None] == indices[None, :]).astype(jnp.int32) + jnp.eye(blocks_all, dtype=jnp.int32)
    for squaring in range(DEPTH.bit_length()):
        linked = jnp.minimum(jnp.dot(linked, linked), 1)
    return linked.astype(jnp.int32)


def block_levels(rng, extent, shards, low, largest):
    def one(axis_at, parts):
        heights = jax.random.uniform(jax.random.fold_in(jax.random.fold_in(rng, 6), axis_at), (parts,), jnp.float32, low / len(shards), largest / len(shards))
        return jnp.repeat(jnp.exp(heights), extent[axis_at] // parts).reshape((-1,) + (1,) * (len(extent) - axis_at - 1))

    loudness = one(*shards[0])
    for cut in shards[1:]:
        loudness = loudness * one(*cut)
    return loudness


def centred(own_key, dims, spread, limit, cuts=(), held_as=jnp.bfloat16):
    drawn = jax.random.normal(own_key, dims, jnp.float32) * spread
    if len(cuts) > 0:
        drawn = block_levels(own_key, dims, cuts, -0.22, 0.18) * drawn
    return jnp.clip(drawn, min=-limit, max=limit).astype(held_as)


def setup_inputs(seed: int = 0) -> dict:
    streams_of = jax.random.split(jax.random.key(seed), 7)
    return {
        "queries": draw_queries(jax.random.fold_in(streams_of[6], 71), 0),
        "latents": draw_latents(jax.random.fold_in(streams_of[6], 71), 0),
        "block_mask": draw_block_mask(jax.random.fold_in(streams_of[6], 71), 0),
        "w_key": centred(streams_of[3], (LATENT, HEADS * NOPE), LATENT ** -0.5, 0.25, ((1, 8),)),
        "w_value": centred(streams_of[4], (LATENT, HEADS * VDIM), LATENT ** -0.5, 0.25, ((1, 8),)),
        "w_out": centred(streams_of[5], (HEADS * VDIM, OUT_COLS), (HEADS * VDIM) ** -0.5, 0.0625, ((0, 8),)),
    }


def rotate(halves_in, places):
    halfway = halves_in.shape[-1] // 2
    freqs_all = 10000.0 ** (-jnp.arange(halfway, dtype=jnp.float32) / halfway)
    angles = places[..., None] * freqs_all
    cosine = jnp.cos(angles)
    sine_part = jnp.sin(angles)
    leading = halves_in[..., :halfway]
    trailing = halves_in[..., halfway:]
    return jnp.concatenate([leading * cosine - trailing * sine_part, trailing * cosine + leading * sine_part], axis=-1)

def reference(queries, latents, block_mask, w_key, w_value, w_out):
    blocks_all = TOKENS // BLOCK
    depths = lax.optimization_barrier(jnp.sum(block_mask, axis=1)).astype(jnp.int32)
    tokens_idx = jnp.arange(TOKENS, dtype=jnp.int32)
    places = (BLOCK * (depths[tokens_idx // BLOCK] - 1) + tokens_idx % BLOCK).astype(jnp.float32)
    shaped = queries.reshape(TOKENS, HEADS, NOPE + ROPE)
    query_nope = shaped[:, :, :NOPE]
    query_rope = rotate(shaped[:, :, NOPE:].astype(jnp.float32), places[:, None]).astype(jnp.bfloat16)
    latent_part = latents[:, :LATENT]
    key_nope = jnp.dot(latent_part, w_key, preferred_element_type=jnp.float32).astype(jnp.bfloat16).reshape(TOKENS, HEADS, NOPE)
    key_vals = jnp.dot(latent_part, w_value, preferred_element_type=jnp.float32).astype(jnp.bfloat16).reshape(TOKENS, HEADS, VDIM)
    key_rope = rotate(latents[:, LATENT:].astype(jnp.float32), places).astype(jnp.bfloat16)
    ancestry = jnp.argsort(-block_mask, axis=1, stable=True)[:, :DEPTH].astype(jnp.int32)
    scaling = 1.0 / math.sqrt(NOPE + ROPE)
    offsets = jnp.arange(BLOCK, dtype=jnp.int32)

    def one_block(block_id):
        chosen = ancestry[block_id]
        present = block_mask[block_id][chosen] == 1
        key_ids = (chosen[:, None] * BLOCK + offsets[None, :]).reshape(-1).astype(jnp.int32)
        query_ids = block_id * BLOCK + offsets
        start_row = (block_id * BLOCK).astype(jnp.int32)
        nope_rows = lax.dynamic_slice_in_dim(query_nope, start_row, BLOCK, 0).astype(jnp.float32)
        rope_rows = lax.dynamic_slice_in_dim(query_rope, start_row, BLOCK, 0).astype(jnp.float32)
        scores = jnp.einsum('qhd,khd->qhk', nope_rows, key_nope[key_ids].astype(jnp.float32))
        scores = (scores + jnp.einsum('qhd,kd->qhk', rope_rows, key_rope[key_ids].astype(jnp.float32))) * scaling
        present_keys = jnp.repeat(present, BLOCK)
        same_block = jnp.repeat(chosen == block_id, BLOCK)
        allowed = present_keys[None, :] & (~same_block[None, :] | (key_ids[None, :] <= query_ids[:, None]))
        allowed = allowed[:, None, :]
        masked = jnp.where(allowed, scores, -jnp.inf)
        highest = lax.optimization_barrier(jnp.max(masked, axis=2, keepdims=True))
        weights = jnp.where(allowed, jnp.exp(scores - highest), 0.0)
        totals = lax.optimization_barrier(jnp.sum(weights, axis=2))
        rounded = lax.optimization_barrier(weights.astype(jnp.bfloat16))
        attended = jnp.einsum('qhk,khd->qhd', rounded.astype(jnp.float32), key_vals[key_ids].astype(jnp.float32))
        return (attended / totals[:, :, None]).astype(jnp.bfloat16)
    heard_all = lax.map(one_block, jnp.arange(blocks_all, dtype=jnp.int32)).reshape(TOKENS, HEADS * VDIM)
    return jnp.dot(heard_all, w_out, preferred_element_type=jnp.float32).astype(jnp.bfloat16)
```

```python
import math
from functools import partial

import numpy as np
import jax
import jax.numpy as jnp
from jax import lax
from jax.experimental import pallas as pl
from jax.experimental.pallas import tpu as pltpu
from jax.sharding import PartitionSpec as P

BLOCK = 128
NOPE = 128
ROPE = 64
VDIM = 128
LATENT = 512
WIDE = 640
SLOTS = 28
UNION = 16
PAIRS = ((2, 1), (3, 0))
QUART = 4 * (NOPE + ROPE)
COLS = 3584
F32 = jnp.float32
BF16 = jnp.bfloat16


def moved(value, dy=0, dx=0, dc=0, dz=0):
    pairs = []
    for y in range(4):
        for x in range(4):
            for c in range(2):
                for z in range(4):
                    place = lambda y, x, c, z: (y * 4 + (x // 2) * 2 + c) * 8 + (x % 2) * 4 + z
                    pairs.append(
                        (
                            place(y, x, c, z),
                            place((y + dy) % 4, (x + dx) % 4, (c + dc) % 2, (z + dz) % 4),
                        )
                    )
    return lax.ppermute(value, ("blk", "uly"), pairs)


def swap_halves(x):
    lane = lax.broadcasted_iota(jnp.int32, x.shape, 1)
    return jnp.where(lane % 64 < 32, pltpu.roll(x, 96, axis=1), pltpu.roll(x, 32, axis=1))


def prologue_kernel(sc, mask_ref, lat_ref, freq_ref, meta_ref, cos_ref, sin_ref, tmp):
    g, xl, z = sc[0], sc[1], sc[2]
    rows = mask_ref[pl.ds(pl.multiple_of(8 * g, 8), 8), :].astype(F32)
    ri = lax.broadcasted_iota(jnp.int32, (8, 128), 0)
    li = lax.broadcasted_iota(jnp.int32, (8, 128), 1)
    upper = (
        lax.broadcasted_iota(jnp.int32, (128, 128), 0) <= lax.broadcasted_iota(jnp.int32, (128, 128), 1)
    ).astype(F32)
    is_self = li == 8 * g + ri
    others = jnp.where(is_self, 0.0, rows)
    row_rank = jnp.dot(others, upper, preferred_element_type=F32)
    ahead = (ri + 8 - (xl * 4 + z)) % 4
    mine = ri // 4 == xl
    in_first = mine & ((ahead == PAIRS[0][0]) | (ahead == PAIRS[0][1]))

    def order(inside):
        wanted = jnp.broadcast_to(inside, (8, 128))
        return wanted, jnp.dot(wanted, upper, preferred_element_type=F32)

    in_a, order_a = order(jnp.max(jnp.where(in_first, rows, 0.0), axis=0, keepdims=True))
    in_b, order_b = order(jnp.max(jnp.where(mine & ~in_first, rows, 0.0), axis=0, keepdims=True))
    own_at = li - (8 * g + 4 * xl)
    is_own = (own_at >= 0) & (own_at < 4)
    needed = jnp.max(jnp.where(mine & ~is_own, rows, 0.0), axis=0, keepdims=True)
    needed, order_all = order(needed)
    slot_of = jnp.where(is_own, own_at.astype(F32) + float(SLOTS), order_all - 1.0)
    place_of = jnp.where(in_first, order_a, order_b) - 1.0
    acc = jnp.where(li == 0, jnp.sum(jnp.where(is_self, place_of, 0.0), axis=1, keepdims=True), 0.0)
    for j in range(1, 8):
        hit = (row_rank == float(j)) & (others > 0.5)
        acc = jnp.where(li == j, jnp.sum(jnp.where(hit, place_of, 0.0), axis=1, keepdims=True), acc)
    depth = jnp.sum(rows, axis=1, keepdims=True)
    acc = jnp.where(li == 8, depth, acc)
    meta_ref[32:40, :] = acc.astype(jnp.int32)
    ci = lax.broadcasted_iota(jnp.int32, (32, 128), 0).astype(F32)
    cl = lax.broadcasted_iota(jnp.int32, (32, 128), 1)
    hit = (slot_of[0:1, :] == ci) & (needed[0:1, :] > 0.5)
    table = jnp.where(cl == 0, jnp.sum(jnp.where(hit, cl.astype(F32), 0.0), axis=1, keepdims=True), 0.0)
    for i, (inside, place) in enumerate(((in_a, order_a), (in_b, order_b))):
        hit = (place[0:1, :] == ci + 1.0) & (inside[0:1, :] > 0.5)
        slots = jnp.sum(jnp.where(hit, slot_of[0:1, :], 0.0), axis=1, keepdims=True)
        table = jnp.where(cl == 2 + i, slots, table)
        table = jnp.where(cl == 4 + i, jnp.max(place[0:1, :], axis=1, keepdims=True), table)
    meta_ref[0:32, :] = table.astype(jnp.int32)

    own = jnp.sum(jnp.where(ri == xl * 4 + z, rows, 0.0), axis=1, keepdims=True)
    own = jnp.sum(own, axis=0, keepdims=True)
    token = lax.broadcasted_iota(jnp.int32, (128, 128), 0).astype(F32)
    angles = (128.0 * (own - 1.0) + token) * freq_ref[0:1, :]
    lane = lax.broadcasted_iota(jnp.int32, (128, 128), 1)
    cosine = jnp.cos(angles)
    sine = jnp.where(lane % 64 < 32, -jnp.sin(angles), jnp.sin(angles))
    cos_ref[...] = cosine
    sin_ref[...] = sine
    rope = lat_ref[:, LATENT:].astype(F32)
    rope = jnp.concatenate([rope, rope], axis=1)
    tmp[:, :LATENT] = lat_ref[:, :LATENT]
    tmp[:, LATENT:] = (rope * cosine + swap_halves(rope) * sine).astype(BF16)


def prologue(sc, block_mask, latents, freq):
    table = jax.ShapeDtypeStruct((128, 128), F32)
    return pl.pallas_call(
        prologue_kernel,
        grid_spec=pltpu.PrefetchScalarGridSpec(
            num_scalar_prefetch=1,
            grid=(),
            in_specs=[pl.BlockSpec(memory_space=pltpu.VMEM)] * 3,
            out_specs=[pl.BlockSpec(memory_space=pltpu.VMEM)] * 4,
        ),
        out_shape=[
            jax.ShapeDtypeStruct((40, 128), jnp.int32),
            table,
            table,
            jax.ShapeDtypeStruct((128, WIDE), BF16),
        ],
        name="prologue",
    )(sc, block_mask, latents, freq)


def query_kernel(sc, x0, x1, x3, cos_ref, sin_ref, own, up, down):
    step = pl.program_id(0)
    cosine, sine = cos_ref[...], sin_ref[...]
    lane = lax.broadcasted_iota(jnp.int32, (128, 128), 1)

    def prepare(x_ref, out):
        for pair in range(2):
            at = 384 * pair
            mid = x_ref[:, at + 128 : at + 256].astype(F32)
            last = x_ref[:, at + 256 : at + 384].astype(F32)
            second = pltpu.roll(jnp.where(lane < 64, last, mid), 64, axis=1)
            rope = jnp.where(lane < 64, mid, last)
            rope = rope * cosine + swap_halves(rope) * sine
            out[:, at : at + 128] = x_ref[:, at : at + 128]
            out[:, at + 128 : at + 256] = second.astype(BF16)
            out[:, at + 256 : at + 384] = rope.astype(BF16)

    @pl.when(step < 4)
    def _():
        prepare(x0, own)
        prepare(x1, up)
        prepare(x3, down)

    @pl.when(step >= 4)
    def _():
        prepare(x1, up)
        prepare(x3, down)


def query_prep(sc, queries, cosine, sine):
    def source(k):
        def index(t, sc):
            xl, z, c = sc[1], sc[2], sc[3]
            ahead, quarter = k, t
            if k in (1, 3):
                ahead = jnp.where(t < 4, k, 2)
                quarter = jnp.where(t < 4, t, t - 4 if k == 1 else t - 2)
            else:
                quarter = jnp.minimum(t, 3)
            zd = (z + ahead) % 4
            own = (xl * 4 + zd) * 2 + quarter
            other = ((1 - xl) * 4 + zd) * 2 + jnp.where(quarter == 2, c, 1 - c)
            return (0, jnp.where(quarter < 2, own, other))

        return pl.BlockSpec((128, QUART), index)

    table = pl.BlockSpec((128, 128), lambda t, sc: (0, 0))
    return pl.pallas_call(
        query_kernel,
        grid_spec=pltpu.PrefetchScalarGridSpec(
            num_scalar_prefetch=1,
            grid=(6,),
            in_specs=[source(k) for k in (0, 1, 3)] + [table, table],
            out_specs=[
                pl.BlockSpec((128, QUART), lambda t, sc: (0, jnp.minimum(t, 3))),
                pl.BlockSpec((128, QUART), lambda t, sc: (0, t)),
                pl.BlockSpec((128, QUART), lambda t, sc: (0, t)),
            ],
        ),
        out_shape=[jax.ShapeDtypeStruct((128, n * QUART), BF16) for n in (4, 6, 6)],
        name="query_prep",
    )(sc, queries, queries, queries, cosine, sine)


def select_kernel(sc, meta, a0, a1, b0, b1, out):
    z, c, y, x = sc[2], sc[3], sc[4], sc[5]
    for slot in range(SLOTS):
        block = meta[slot, 0]
        ze = (z + 4 - block % 4) % 4
        xl = (block // 4) % 2
        core = (block // 8) % 2
        xe = (x + 4 - ((block // 16) % 2 * 2 + xl)) % 4
        ye = (y + 4 - block // 32) % 4
        at_a = (ye * 4 + xe) * 4 + ze
        at_b = (xe * 4 + ye) * 4 + ze

        @pl.when(core == c)
        def _():
            out[slot, 0:16, :] = a0[at_a]
            out[slot, 16:32, :] = b0[at_b]

        @pl.when(core != c)
        def _():
            out[slot, 0:16, :] = a1[at_a]
            out[slot, 16:32, :] = b1[at_b]


def select(sc, meta, a0, a1, b0, b1):
    return pl.pallas_call(
        select_kernel,
        grid_spec=pltpu.PrefetchScalarGridSpec(
            num_scalar_prefetch=2,
            grid=(),
            in_specs=[pl.BlockSpec(memory_space=pltpu.VMEM)] * 4,
            out_specs=pl.BlockSpec(memory_space=pltpu.VMEM),
        ),
        out_shape=jax.ShapeDtypeStruct((SLOTS, 32, WIDE), BF16),
        compiler_params=pltpu.CompilerParams(vmem_limit_bytes=40 * 2**20),
        name="select_blocks",
    )(sc, meta, a0, a1, b0, b1)


def attend_kernel(which, sc, meta, *refs):
    q_refs, refs = refs[:3], refs[3:]
    gathered, owns, refs = refs[0:5], refs[5:9], refs[9:]
    wks, wvs, heard = refs[0:3], refs[3:6], refs[6]
    rows_all, wk, wv, keys, vals, row_sems, w_sems = refs[7:]
    step = pl.program_id(0)
    xl, z = sc[1], sc[2]
    count = meta[0, 4 + which]

    def weight_copies(t):
        part = 0 if t < 2 else t - 1
        copies = []
        for i, (ws, w) in enumerate(((wks, wk), (wvs, wv))):
            source = ws[part]
            if t < 2:
                source = source.at[:, pl.ds(512 * t, 512)]
            copies.append(pltpu.make_async_copy(source, w.at[t], w_sems.at[t, i]))
        return copies

    def row_copies(u):
        slot = meta[u, 2 + which]
        ends = ((0, 32), (32, 32), (64, 16), (80, 16), (96, 32))

        def parts(sources, at):
            return [
                pltpu.make_async_copy(s.at[at], rows_all.at[u, pl.ds(first, n), :], row_sems.at[u, i])
                for i, (s, (first, n)) in enumerate(zip(sources, ends))
            ]

        def each(do):
            @pl.when(slot < SLOTS)
            def _():
                for copy in parts(gathered, jnp.minimum(slot, SLOTS - 1)):
                    do(copy)

            for k, own_rows in enumerate(owns):

                @pl.when(slot == SLOTS + (z + 4 - k) % 4)
                def _(own_rows=own_rows):
                    do(pltpu.make_async_copy(own_rows, rows_all.at[u], row_sems.at[u, 0]))

        return each

    @pl.when(step == 0)
    def _():
        @pl.loop(0, count)
        def _(u):
            row_copies(u)(lambda copy: copy.start())

        for t in range(4):
            for copy in weight_copies(t):
                copy.start()

        @pl.loop(0, count)
        def _(u):
            row_copies(u)(lambda copy: copy.wait())

    for t in range(4):

        @pl.when(step == t)
        def _(t=t):
            for copy in weight_copies(t):
                copy.wait()

    for chunk in range(UNION // 4):

        @pl.when(chunk * 4 < count)
        def _(chunk=chunk):
            at = slice(chunk * 4, chunk * 4 + 4)
            latent = rows_all[at, :, :LATENT].reshape(512, LATENT)
            keys[at] = jnp.dot(latent, wk[step], preferred_element_type=F32).astype(BF16).reshape(4, 128, 512)
            vals[at] = jnp.dot(latent, wv[step], preferred_element_type=F32).astype(BF16).reshape(4, 128, 512)

    factor = math.log2(math.e) / math.sqrt(NOPE + ROPE)
    lane = lax.broadcasted_iota(jnp.int32, (128, 128), 1)
    row = lax.broadcasted_iota(jnp.int32, (128, 128), 0)
    causal = lane <= row

    for b in range(2):
        line = 32 + xl * 4 + (z + PAIRS[which][b]) % 4
        depth = meta[line, 8]

        def run(tiles, b=b, line=line, depth=depth):
            def q_cols(first):
                part = q_refs[b if which else 2 * b][:, first : first + 128]
                if which == 0 and b == 0:
                    part = jnp.where(step < 2, part, q_refs[1][:, first : first + 128])
                return part

            at = [meta[line, j] for j in range(tiles)]
            for head in range(4):
                first = 384 * (head // 2)
                cols = slice(head * 128, head * 128 + 128)
                nope = q_cols(first + 128 * (head % 2))
                mine = (lane < 64) if head % 2 == 0 else (lane >= 64)
                rope = jnp.where(mine, q_cols(first + 256).astype(F32), 0.0)
                query = jnp.concatenate([nope, rope.astype(BF16)], axis=1)
                key = jnp.concatenate(
                    [
                        jnp.concatenate([keys[a, :, cols], rows_all[a, :, LATENT:]], axis=1)
                        for a in at
                    ],
                    axis=0,
                )
                value = jnp.concatenate([vals[a, :, cols] for a in at], axis=0)
                scores = lax.dot_general(query, key, (((1,), (1,)), ((), ())), preferred_element_type=F32)
                scores = [scores[:, 128 * j : 128 * j + 128] for j in range(tiles)]
                scores[0] = jnp.where(causal, scores[0], -jnp.inf)
                scores[-1] = jnp.where(tiles - 1 < depth, scores[-1], -jnp.inf)
                peak = scores[0]
                for s in scores[1:]:
                    peak = jnp.maximum(peak, s)
                peak = jnp.max(peak, axis=1, keepdims=True)
                weights = [jnp.exp2((s - peak) * factor) for s in scores]
                total = weights[0]
                for w in weights[1:]:
                    total = total + w
                total = jnp.sum(total, axis=1, keepdims=True)
                probs = jnp.concatenate([w.astype(BF16) for w in weights], axis=1)
                found = jnp.dot(probs, value, preferred_element_type=F32)
                heard[b * 128 : b * 128 + 128, cols] = (found / total).astype(BF16)

        for tiles in (2, 4, 6, 8):

            @pl.when((depth == tiles) | (depth == tiles - 1))
            def _(run=run, tiles=tiles):
                run(tiles)


def attend(which, sc, meta, queries, pieces, wk, wv):
    query = pl.BlockSpec((128, QUART), lambda t, sc, m: (0, t))
    if which == 0:
        q_specs = [
            pl.BlockSpec((128, QUART), lambda t, sc, m: (0, jnp.minimum(t, 1))),
            pl.BlockSpec((128, QUART), lambda t, sc, m: (0, jnp.maximum(t - 2, 0))),
            query,
        ]
    else:
        q_specs = [query, query, pl.BlockSpec((128, QUART), lambda t, sc, m: (0, 0))]
    hbm = pl.BlockSpec(memory_space=pltpu.HBM)
    return pl.pallas_call(
        partial(attend_kernel, which),
        grid_spec=pltpu.PrefetchScalarGridSpec(
            num_scalar_prefetch=2,
            grid=(4,),
            in_specs=q_specs + [hbm] * (len(pieces) + 6),
            out_specs=pl.BlockSpec((256, 512), lambda t, sc, m: (0, t)),
            scratch_shapes=[
                pltpu.VMEM((UNION, 128, WIDE), BF16),
                pltpu.VMEM((4, LATENT, 512), BF16),
                pltpu.VMEM((4, LATENT, 512), BF16),
                pltpu.VMEM((UNION, 128, 512), BF16),
                pltpu.VMEM((UNION, 128, 512), BF16),
                pltpu.SemaphoreType.DMA((UNION, 5)),
                pltpu.SemaphoreType.DMA((4, 2)),
            ],
        ),
        out_shape=jax.ShapeDtypeStruct((256, 2048), BF16),
        compiler_params=pltpu.CompilerParams(vmem_limit_bytes=40 * 2**20),
        name="attend_%d" % which,
    )(sc, meta, *queries, *pieces, *wk, *wv)


def project_kernel(heard, *refs):
    ws, outs = refs[:5], refs[5:]
    at = 0
    total = None
    for w in ws:
        n = w.shape[0]
        part = jnp.dot(heard[:, at : at + n], w[...], preferred_element_type=F32)
        total = part if total is None else total + part
        at += n
    total = total.astype(BF16)
    outs[0][...] = total[:128]
    outs[1][...] = total[128:]


def project(heard, w_parts):
    return pl.pallas_call(
        project_kernel,
        grid=(COLS // 512,),
        in_specs=[pl.BlockSpec((256, 2048), lambda n: (0, 0))]
        + [pl.BlockSpec((w.shape[0], 512), lambda n: (0, n)) for w in w_parts],
        out_specs=[pl.BlockSpec((128, 512), lambda n: (0, n))] * 2,
        out_shape=[jax.ShapeDtypeStruct((128, COLS), BF16)] * 2,
        compiler_params=pltpu.CompilerParams(vmem_limit_bytes=32 * 2**20),
        name="project",
    )(heard, *w_parts)


def gather_ring(value, axis):
    one = moved(value, **{axis: 1})
    three = moved(value, **{axis: 3})
    two = moved(value, **{axis: 2})
    return jnp.concatenate([value, one, two, three], axis=0)


def local(queries, latents, block_mask, w_key, w_value, w_out):
    g = lax.axis_index("blk").astype(jnp.int32)
    u = lax.axis_index("uly").astype(jnp.int32)
    c, y, xl, z = g % 2, g // 4, u // 4, u % 4
    x = (g // 2) % 2 * 2 + xl
    sc = jnp.stack([g, xl, z, c, y, x])
    freq = np.float32(10000.0) ** (-np.arange(32, dtype=np.float32) / np.float32(32))
    freq = jnp.asarray(np.tile(freq[None, :], (8, 4)))

    meta, cosine, sine, block = prologue(sc, block_mask, latents, freq)
    owns = [block, moved(block, dz=1), moved(block, dz=2), moved(block, dz=3)]
    q_own, q_up, q_down = query_prep(sc, queries, cosine, sine)
    mine = jnp.stack([lax.dynamic_slice_in_dim(own, 32 * z, 32, 0) for own in owns])
    half_a, half_b = mine[:, :16], mine[:, 16:]
    half_a, half_b, q_up, q_down = lax.optimization_barrier((half_a, half_b, q_up, q_down))

    q_up, q_down = moved(q_up, dz=1), moved(q_down, dz=3)
    far_up = moved(q_up[:, 4 * QUART :], dz=1)
    far_down = moved(q_down[:, 4 * QUART :], dz=3)
    half_a = gather_ring(half_a, "dx")
    half_b = gather_ring(half_b, "dy")

    half_a, half_b, w_key_now, w_value_now = lax.optimization_barrier((half_a, half_b, w_key, w_value))
    wk_half = lax.dynamic_slice_in_dim(w_key_now, c * 512, 512, 1)
    wv_half = lax.dynamic_slice_in_dim(w_value_now, c * 512, 512, 1)
    wk_m, wv_m = moved(wk_half, dx=1), moved(wv_half, dx=3)

    half_a = gather_ring(half_a, "dy")
    half_b = gather_ring(half_b, "dx")
    half_a, half_b, w_out_now, far_up, far_down, wk_m, wv_m = lax.optimization_barrier(
        (half_a, half_b, w_out, far_up, far_down, wk_m, wv_m)
    )
    other_a = moved(half_a, dc=1)
    other_b = moved(half_b, dc=1)
    wk_t, wv_t = moved(wk_m, dc=1), moved(wv_m, dc=1)
    wo_one = lax.dynamic_slice_in_dim(w_out_now, c * 512, 256, 0)
    wo_two = lax.dynamic_slice_in_dim(w_out_now, c * 512 + 256, 256, 0)
    wo_m1, wo_m2 = moved(wo_one, dx=1), moved(wo_two, dx=3)
    chosen = select(sc, meta, half_a, other_a, half_b, other_b)
    back, ahead = moved(chosen, dz=1), moved(chosen, dz=3)
    far_a = moved(back[:, :16], dz=1)
    far_b = moved(ahead[:, 16:], dz=3)

    pieces = (chosen, back, far_a, far_b, ahead, *owns)
    wk, wv = (w_key, wk_m, wk_t), (w_value, wv_m, wv_t)
    heard = attend(0, sc, meta, (far_up, far_down, q_down), pieces, wk, wv)
    heard, wo_m1, wo_m2 = lax.optimization_barrier((heard, wo_m1, wo_m2))
    wo_t1, wo_t2 = moved(wo_m1, dc=1), moved(wo_m2, dc=1)
    w_parts = (w_out, wo_m1, wo_m2, wo_t1, wo_t2)
    out2, out1 = project(heard, w_parts)
    out2, out1, q_own = lax.optimization_barrier((out2, out1, q_own))
    got2, got1 = moved(out2, dz=2), moved(out1, dz=1)
    heard = attend(1, sc, meta, (q_up, q_own, q_own), pieces, wk, wv)
    heard, got1, got2 = lax.optimization_barrier((heard, got1, got2))
    out3, out0 = project(heard, w_parts)
    got3 = moved(out3, dz=3)
    return (out0.astype(F32) + got1.astype(F32) + got2.astype(F32) + got3.astype(F32)).astype(BF16)


def solution(mesh):
    in_specs = (
        P(("blk", "uly"), None),
        P(("blk", "uly"), None),
        P(),
        P(None, "uly"),
        P(None, "uly"),
        P("uly", None),
    )
    out_specs = P(("blk", "uly"), None)
    return jax.shard_map(local, mesh=mesh, in_specs=in_specs, out_specs=out_specs, check_vma=False)
```

```python
import math
from functools import partial

import numpy as np
import jax
import jax.numpy as jnp
from jax import lax
from jax.experimental import pallas as pl
from jax.experimental.pallas import tpu as pltpu
from jax.sharding import PartitionSpec as P

BLOCK = 128
NOPE = 128
ROPE = 64
VDIM = 128
LATENT = 512
WIDE = 640
SLOTS = 28
FIRST = 20
UNION = 16
PAIRS = ((2, 0), (1, 3))
QUART = 4 * (NOPE + ROPE)
COLS = 3584
F32 = jnp.float32
BF16 = jnp.bfloat16


def moved(value, dy=0, dx=0, dc=0, dz=0):
    pairs = []
    for y in range(4):
        for x in range(4):
            for c in range(2):
                for z in range(4):
                    place = lambda y, x, c, z: (y * 4 + (x // 2) * 2 + c) * 8 + (x % 2) * 4 + z
                    pairs.append(
                        (
                            place(y, x, c, z),
                            place((y + dy) % 4, (x + dx) % 4, (c + dc) % 2, (z + dz) % 4),
                        )
                    )
    return lax.ppermute(value, ("blk", "uly"), pairs)


def swap_halves(x):
    lane = lax.broadcasted_iota(jnp.int32, x.shape, 1)
    return jnp.where(lane % 64 < 32, pltpu.roll(x, 96, axis=1), pltpu.roll(x, 32, axis=1))


def prologue_kernel(sc, mask_ref, lat_ref, freq_ref, meta_ref, cos_ref, sin_ref, tmp):
    g, xl, z = sc[0], sc[1], sc[2]
    rows = mask_ref[pl.ds(pl.multiple_of(8 * g, 8), 8), :].astype(F32)
    ri = lax.broadcasted_iota(jnp.int32, (8, 128), 0)
    li = lax.broadcasted_iota(jnp.int32, (8, 128), 1)
    upper = (
        lax.broadcasted_iota(jnp.int32, (128, 128), 0) <= lax.broadcasted_iota(jnp.int32, (128, 128), 1)
    ).astype(F32)
    is_self = li == 8 * g + ri
    others = jnp.where(is_self, 0.0, rows)
    row_rank = jnp.dot(others, upper, preferred_element_type=F32)
    ahead = (ri + 8 - (xl * 4 + z)) % 4
    mine = ri // 4 == xl
    in_first = mine & ((ahead == PAIRS[0][0]) | (ahead == PAIRS[0][1]))

    def order(inside):
        wanted = jnp.broadcast_to(inside, (8, 128))
        return wanted, jnp.dot(wanted, upper, preferred_element_type=F32)

    in_a, order_a = order(jnp.max(jnp.where(in_first, rows, 0.0), axis=0, keepdims=True))
    in_b, order_b = order(jnp.max(jnp.where(mine & ~in_first, rows, 0.0), axis=0, keepdims=True))
    own_at = li - (8 * g + 4 * xl)
    is_own = (own_at >= 0) & (own_at < 4)
    needed = jnp.max(jnp.where(mine & ~is_own, rows, 0.0), axis=0, keepdims=True)
    needed, order_all = order(needed)
    slot_of = jnp.where(is_own, own_at.astype(F32) + float(SLOTS), order_all - 1.0)
    place_of = jnp.where(in_first, order_a, order_b) - 1.0
    acc = jnp.where(li == 0, jnp.sum(jnp.where(is_self, place_of, 0.0), axis=1, keepdims=True), 0.0)
    for j in range(1, 8):
        hit = (row_rank == float(j)) & (others > 0.5)
        acc = jnp.where(li == j, jnp.sum(jnp.where(hit, place_of, 0.0), axis=1, keepdims=True), acc)
    depth = jnp.sum(rows, axis=1, keepdims=True)
    acc = jnp.where(li == 8, depth, acc)
    meta_ref[32:40, :] = acc.astype(jnp.int32)
    ci = lax.broadcasted_iota(jnp.int32, (32, 128), 0).astype(F32)
    cl = lax.broadcasted_iota(jnp.int32, (32, 128), 1)
    hit = (slot_of[0:1, :] == ci) & (needed[0:1, :] > 0.5)
    table = jnp.where(cl == 0, jnp.sum(jnp.where(hit, cl.astype(F32), 0.0), axis=1, keepdims=True), 0.0)
    for i, (inside, place) in enumerate(((in_a, order_a), (in_b, order_b))):
        hit = (place[0:1, :] == ci + 1.0) & (inside[0:1, :] > 0.5)
        slots = jnp.sum(jnp.where(hit, slot_of[0:1, :], 0.0), axis=1, keepdims=True)
        table = jnp.where(cl == 2 + i, slots, table)
        table = jnp.where(cl == 4 + i, jnp.max(place[0:1, :], axis=1, keepdims=True), table)
    group = lax.broadcasted_iota(jnp.int32, (128, 128), 0) // 4
    apart = group != lax.broadcasted_iota(jnp.int32, (128, 128), 1) // 4
    links = jnp.where(apart, mask_ref[...].astype(F32), 0.0)
    most = jnp.sum(jnp.max(links.reshape(32, 4, 128), axis=1), axis=1, keepdims=True)
    most = jnp.max(most, axis=0, keepdims=True)
    table = jnp.where(cl == 6, most, table)
    meta_ref[0:32, :] = table.astype(jnp.int32)

    own = jnp.sum(jnp.where(ri == xl * 4 + z, rows, 0.0), axis=1, keepdims=True)
    own = jnp.sum(own, axis=0, keepdims=True)
    token = lax.broadcasted_iota(jnp.int32, (128, 128), 0).astype(F32)
    angles = (128.0 * (own - 1.0) + token) * freq_ref[0:1, :]
    lane = lax.broadcasted_iota(jnp.int32, (128, 128), 1)
    cosine = jnp.cos(angles)
    sine = jnp.where(lane % 64 < 32, -jnp.sin(angles), jnp.sin(angles))
    cos_ref[...] = cosine
    sin_ref[...] = sine
    rope = lat_ref[:, LATENT:].astype(F32)
    rope = jnp.concatenate([rope, rope], axis=1)
    tmp[:, :LATENT] = lat_ref[:, :LATENT]
    tmp[:, LATENT:] = (rope * cosine + swap_halves(rope) * sine).astype(BF16)


def prologue(sc, block_mask, latents, freq):
    table = jax.ShapeDtypeStruct((128, 128), F32)
    return pl.pallas_call(
        prologue_kernel,
        grid_spec=pltpu.PrefetchScalarGridSpec(
            num_scalar_prefetch=1,
            grid=(),
            in_specs=[pl.BlockSpec(memory_space=pltpu.VMEM)] * 3,
            out_specs=[pl.BlockSpec(memory_space=pltpu.VMEM)] * 4,
        ),
        out_shape=[
            jax.ShapeDtypeStruct((40, 128), jnp.int32),
            table,
            table,
            jax.ShapeDtypeStruct((128, WIDE), BF16),
        ],
        name="prologue",
    )(sc, block_mask, latents, freq)


def query_kernel(sc, x0, x1, x3, cos_ref, sin_ref, own, up, down):
    step = pl.program_id(0)
    cosine, sine = cos_ref[...], sin_ref[...]
    lane = lax.broadcasted_iota(jnp.int32, (128, 128), 1)

    def prepare(x_ref, out):
        for pair in range(2):
            at = 384 * pair
            mid = x_ref[:, at + 128 : at + 256].astype(F32)
            last = x_ref[:, at + 256 : at + 384].astype(F32)
            second = pltpu.roll(jnp.where(lane < 64, last, mid), 64, axis=1)
            rope = jnp.where(lane < 64, mid, last)
            rope = rope * cosine + swap_halves(rope) * sine
            out[:, at : at + 128] = x_ref[:, at : at + 128]
            out[:, at + 128 : at + 256] = second.astype(BF16)
            out[:, at + 256 : at + 384] = rope.astype(BF16)

    @pl.when(step < 4)
    def _():
        prepare(x0, own)
        prepare(x1, up)
        prepare(x3, down)

    @pl.when(step >= 4)
    def _():
        prepare(x1, up)
        prepare(x3, down)


def query_prep(sc, queries, cosine, sine):
    def source(k):
        def index(t, sc):
            xl, z, c = sc[1], sc[2], sc[3]
            ahead, quarter = k, t
            if k in (1, 3):
                ahead = jnp.where(t < 4, k, 2)
                quarter = jnp.where(t < 4, t, t - 4 if k == 1 else t - 2)
            else:
                quarter = jnp.minimum(t, 3)
            zd = (z + ahead) % 4
            own = (xl * 4 + zd) * 2 + quarter
            other = ((1 - xl) * 4 + zd) * 2 + jnp.where(quarter == 2, c, 1 - c)
            return (0, jnp.where(quarter < 2, own, other))

        return pl.BlockSpec((128, QUART), index)

    table = pl.BlockSpec((128, 128), lambda t, sc: (0, 0))
    return pl.pallas_call(
        query_kernel,
        grid_spec=pltpu.PrefetchScalarGridSpec(
            num_scalar_prefetch=1,
            grid=(6,),
            in_specs=[source(k) for k in (0, 1, 3)] + [table, table],
            out_specs=[
                pl.BlockSpec((128, QUART), lambda t, sc: (0, jnp.minimum(t, 3))),
                pl.BlockSpec((128, QUART), lambda t, sc: (0, t)),
                pl.BlockSpec((128, QUART), lambda t, sc: (0, t)),
            ],
        ),
        out_shape=[jax.ShapeDtypeStruct((128, n * QUART), BF16) for n in (4, 6, 6)],
        name="query_prep",
    )(sc, queries, queries, queries, cosine, sine)


def select_kernel(sc, meta, a0, a1, b0, b1, low, high, sems):
    z, c, y, x = sc[2], sc[3], sc[4], sc[5]

    def copies(slot):
        block = meta[slot, 0]
        ze = (z + 4 - block % 4) % 4
        xl = (block // 4) % 2
        core = (block // 8) % 2
        xe = (x + 4 - ((block // 16) % 2 * 2 + xl)) % 4
        ye = (y + 4 - block // 32) % 4
        at_a = (ye * 4 + xe) * 4 + ze
        at_b = (xe * 4 + ye) * 4 + ze

        out, at = (low, slot) if slot < FIRST else (high, slot - FIRST)

        def pair(a, b):
            return [
                pltpu.make_async_copy(a.at[at_a], out.at[at, pl.ds(0, 16), :], sems.at[slot, 0]),
                pltpu.make_async_copy(b.at[at_b], out.at[at, pl.ds(16, 16), :], sems.at[slot, 1]),
            ]

        return core, pair

    for slot in range(SLOTS):
        core, pair = copies(slot)

        @pl.when(core == c)
        def _(pair=pair):
            for copy in pair(a0, b0):
                copy.start()

        @pl.when(core != c)
        def _(pair=pair):
            for copy in pair(a1, b1):
                copy.start()

    for slot in range(SLOTS):
        core, pair = copies(slot)
        for copy in pair(a0, b0):
            copy.wait()


def select(sc, meta, a0, a1, b0, b1):
    return pl.pallas_call(
        select_kernel,
        grid_spec=pltpu.PrefetchScalarGridSpec(
            num_scalar_prefetch=2,
            grid=(),
            in_specs=[pl.BlockSpec(memory_space=pl.ANY)] * 4,
            out_specs=[pl.BlockSpec(memory_space=pltpu.VMEM)] * 2,
            scratch_shapes=[pltpu.SemaphoreType.DMA((SLOTS, 2))],
        ),
        out_shape=[
            jax.ShapeDtypeStruct((FIRST, 32, WIDE), BF16),
            jax.ShapeDtypeStruct((SLOTS - FIRST, 32, WIDE), BF16),
        ],
        name="select_blocks",
    )(sc, meta, a0, a1, b0, b1)


def attend_kernel(which, sc, meta, *refs):
    q_refs, refs = refs[:3], refs[3:]
    low, high, owns, refs = refs[0:5], refs[5:10], refs[10:14], refs[14:]
    wks, wvs, heard = refs[0:3], refs[3:6], refs[6]
    rows_all, wk, wv, keys, vals, ropes, row_sems, w_sems = refs[7:]
    step = pl.program_id(0)
    xl, z = sc[1], sc[2]
    count = meta[0, 4 + which]

    def weight_copies(t):
        part = 0 if t < 2 else t - 1
        copies = []
        for i, (ws, w) in enumerate(((wks, wk), (wvs, wv))):
            source = ws[part]
            if t < 2:
                source = source.at[:, pl.ds(512 * t, 512)]
            copies.append(pltpu.make_async_copy(source, w.at[t], w_sems.at[t, i]))
        return copies

    def row_copies(u):
        slot = meta[u, 2 + which]
        ends = ((0, 32), (32, 32), (64, 16), (80, 16), (96, 32))

        def parts(sources, at):
            return [
                pltpu.make_async_copy(s.at[at], rows_all.at[u, pl.ds(first, n), :], row_sems.at[u, i])
                for i, (s, (first, n)) in enumerate(zip(sources, ends))
            ]

        def each(do):
            @pl.when(slot < FIRST)
            def _():
                for copy in parts(low, jnp.minimum(slot, FIRST - 1)):
                    do(copy)

            @pl.when((slot >= FIRST) & (slot < SLOTS))
            def _():
                for copy in parts(high, jnp.clip(slot - FIRST, 0, SLOTS - FIRST - 1)):
                    do(copy)

            for k, own_rows in enumerate(owns):

                @pl.when(slot == SLOTS + (z + 4 - k) % 4)
                def _(own_rows=own_rows):
                    do(pltpu.make_async_copy(own_rows, rows_all.at[u], row_sems.at[u, 0]))

        return each

    @pl.when(step == 0)
    def _():
        @pl.loop(0, count)
        def _(u):
            row_copies(u)(lambda copy: copy.start())

        for t in range(4):
            for copy in weight_copies(t):
                copy.start()

        @pl.loop(0, count)
        def _(u):
            row_copies(u)(lambda copy: copy.wait())
            ropes[u] = rows_all[u, :, LATENT:].T

    for t in range(4):

        @pl.when(step == t)
        def _(t=t):
            for copy in weight_copies(t):
                copy.wait()

    for chunk in range(UNION // 4):

        @pl.when(chunk * 4 < count)
        def _(chunk=chunk):
            at = slice(chunk * 4, chunk * 4 + 4)
            latent = rows_all[at, :, :LATENT].reshape(512, LATENT)
            key = jnp.dot(latent, wk[step], preferred_element_type=F32).astype(BF16)
            for i in range(4):
                keys[chunk * 4 + i] = key[128 * i : 128 * i + 128].T
            vals[at] = jnp.dot(latent, wv[step], preferred_element_type=F32).astype(BF16).reshape(4, 128, 512)

    factor = math.log2(math.e) / math.sqrt(NOPE + ROPE)
    lane = lax.broadcasted_iota(jnp.int32, (128, 128), 1)
    row = lax.broadcasted_iota(jnp.int32, (128, 128), 0)
    causal = lane <= row

    for b in range(2):
        line = 32 + xl * 4 + (z + PAIRS[which][b]) % 4
        depth = meta[line, 8]

        def run(tiles, b=b, line=line, depth=depth):
            def q_cols(first):
                part = q_refs[b if which else 2 * b][:, first : first + 128]
                if which == 0 and b == 0:
                    part = jnp.where(step < 2, part, q_refs[1][:, first : first + 128])
                return part

            at = [meta[line, j] for j in range(tiles)]
            for pair in range(2):
                first = 384 * pair
                both = slice(pair * 256, pair * 256 + 256)
                value = jnp.concatenate([vals[a, :, both] for a in at], axis=0)
                rope_all = q_cols(first + 256).astype(F32)
                probs, totals = [], []
                for half in range(2):
                    cols = slice(pair * 256 + half * 128, pair * 256 + half * 128 + 128)
                    mine = (lane < 64) if half == 0 else (lane >= 64)
                    rope = jnp.where(mine, rope_all, 0.0)
                    query = jnp.concatenate([q_cols(first + 128 * half), rope.astype(BF16)], axis=1)
                    key = jnp.concatenate(
                        [jnp.concatenate([keys[a, cols, :], ropes[a]], axis=0) for a in at],
                        axis=1,
                    )
                    scores = jnp.dot(query, key, preferred_element_type=F32)
                    scores = [scores[:, 128 * j : 128 * j + 128] for j in range(tiles)]
                    scores[0] = jnp.where(causal, scores[0], -jnp.inf)
                    scores[-1] = jnp.where(tiles - 1 < depth, scores[-1], -jnp.inf)
                    peak = scores[0]
                    for s in scores[1:]:
                        peak = jnp.maximum(peak, s)
                    peak = jnp.max(peak, axis=1, keepdims=True)
                    weights = [jnp.exp2((s - peak) * factor) for s in scores]
                    total = weights[0]
                    for w in weights[1:]:
                        total = total + w
                    totals.append(jnp.sum(total, axis=1, keepdims=True))
                    probs.append(jnp.concatenate([w.astype(BF16) for w in weights], axis=1))
                found = jnp.dot(jnp.concatenate(probs, axis=0), value, preferred_element_type=F32)
                for half in range(2):
                    cols = slice(pair * 256 + half * 128, pair * 256 + half * 128 + 128)
                    part = found[half * 128 : half * 128 + 128, half * 128 : half * 128 + 128]
                    heard[b * 128 : b * 128 + 128, cols] = (part / totals[half]).astype(BF16)

        for tiles in (2, 4, 6, 8):

            @pl.when((depth == tiles) | (depth == tiles - 1))
            def _(run=run, tiles=tiles):
                run(tiles)


def attend(which, sc, meta, queries, pieces, wk, wv):
    query = pl.BlockSpec((128, QUART), lambda t, sc, m: (0, t))
    if which == 0:
        q_specs = [
            pl.BlockSpec((128, QUART), lambda t, sc, m: (0, jnp.minimum(t, 1))),
            pl.BlockSpec((128, QUART), lambda t, sc, m: (0, jnp.maximum(t - 2, 0))),
            query,
        ]
    else:
        q_specs = [query, query, pl.BlockSpec((128, QUART), lambda t, sc, m: (0, 0))]
    hbm = pl.BlockSpec(memory_space=pltpu.HBM)
    return pl.pallas_call(
        partial(attend_kernel, which),
        grid_spec=pltpu.PrefetchScalarGridSpec(
            num_scalar_prefetch=2,
            grid=(4,),
            in_specs=q_specs + [hbm] * (len(pieces) + 6),
            out_specs=pl.BlockSpec((256, 512), lambda t, sc, m: (0, t)),
            scratch_shapes=[
                pltpu.VMEM((UNION, 128, WIDE), BF16),
                pltpu.VMEM((4, LATENT, 512), BF16),
                pltpu.VMEM((4, LATENT, 512), BF16),
                pltpu.VMEM((UNION, 512, 128), BF16),
                pltpu.VMEM((UNION, 128, 512), BF16),
                pltpu.VMEM((UNION, 128, 128), BF16),
                pltpu.SemaphoreType.DMA((UNION, 5)),
                pltpu.SemaphoreType.DMA((4, 2)),
            ],
        ),
        out_shape=pltpu.HBM((256, 2048), BF16),
        compiler_params=pltpu.CompilerParams(vmem_limit_bytes=40 * 2**20),
        name="attend_%d" % which,
    )(sc, meta, *[pltpu.with_memory_space_constraint(a, pltpu.HBM) for a in (*queries, *pieces, *wk, *wv)])


def project_kernel(last, heard, *refs):
    ws, refs = refs[:5], refs[5:]
    step = pl.program_id(0)
    w = jnp.concatenate([w[...] for w in ws], axis=0)
    total = jnp.dot(heard[...], w, preferred_element_type=F32)
    if last:
        above, below, up, down = refs
        up[...] = (total[:128] + jnp.where(step < 2, above[...].astype(F32), 0.0)).astype(BF16)
        down[...] = (total[128:] + jnp.where(step < 2, 0.0, below[...].astype(F32))).astype(BF16)
    else:
        left, right, own = refs
        far = total[:128].astype(BF16)
        own[...] = total[128:].astype(BF16)

        @pl.when(step < 2)
        def _():
            left[...] = far

        @pl.when(step >= 2)
        def _():
            right[...] = far


def project(heard, w_parts, received=()):
    last = len(received) > 0
    cols = COLS // 4
    each = pl.BlockSpec((128, cols), lambda n: (0, n))
    left = pl.BlockSpec((128, cols), lambda n: (0, jnp.minimum(n, 1)))
    right = pl.BlockSpec((128, cols), lambda n: (0, jnp.maximum(n - 2, 0)))
    whole = jax.ShapeDtypeStruct((128, COLS), BF16)
    half = jax.ShapeDtypeStruct((128, COLS // 2), BF16)
    return pl.pallas_call(
        partial(project_kernel, last),
        grid=(4,),
        in_specs=[pl.BlockSpec((256, 2048), lambda n: (0, 0))]
        + [pl.BlockSpec((w.shape[0], cols), lambda n: (0, n)) for w in w_parts]
        + [left, right] * last,
        out_specs=[each, each] if last else [left, right, each],
        out_shape=[whole, whole] if last else [half, half, whole],
        compiler_params=pltpu.CompilerParams(vmem_limit_bytes=32 * 2**20),
        name="project",
    )(pltpu.with_memory_space_constraint(heard, pltpu.HBM), *w_parts, *received)


def gather_ring(value, axis):
    one = moved(value, **{axis: 1})
    three = moved(value, **{axis: 3})
    two = moved(value, **{axis: 2})
    return jnp.concatenate([value, one, two, three], axis=0)


def local(queries, latents, block_mask, w_key, w_value, w_out):
    g = lax.axis_index("blk").astype(jnp.int32)
    u = lax.axis_index("uly").astype(jnp.int32)
    c, y, xl, z = g % 2, g // 4, u // 4, u % 4
    x = (g // 2) % 2 * 2 + xl
    sc = jnp.stack([g, xl, z, c, y, x])
    freq = np.float32(10000.0) ** (-np.arange(32, dtype=np.float32) / np.float32(32))
    freq = jnp.asarray(np.tile(freq[None, :], (8, 4)))

    meta, cosine, sine, block = prologue(sc, block_mask, latents, freq)
    owns = [block, moved(block, dz=1), moved(block, dz=2), moved(block, dz=3)]
    q_own, q_up, q_down = query_prep(sc, queries, cosine, sine)
    mine = jnp.stack([lax.dynamic_slice_in_dim(own, 32 * z, 32, 0) for own in owns])
    half_a, half_b = mine[:, :16], mine[:, 16:]
    wk_m = moved(lax.dynamic_slice_in_dim(w_key, c * 512, 512, 1), dx=1)
    wv_m = moved(lax.dynamic_slice_in_dim(w_value, c * 512, 512, 1), dx=3)
    half_a, half_b, q_up, q_down, wk_m, wv_m = lax.optimization_barrier(
        (half_a, half_b, q_up, q_down, wk_m, wv_m)
    )

    q_up, q_down = moved(q_up, dz=1), moved(q_down, dz=3)
    half_a = gather_ring(half_a, "dx")
    half_b = gather_ring(half_b, "dy")

    half_a, half_b = lax.optimization_barrier((half_a, half_b))
    half_a = gather_ring(half_a, "dy")
    half_b = gather_ring(half_b, "dx")
    wo_one = lax.dynamic_slice_in_dim(w_out, c * 512, 256, 0)
    wo_two = lax.dynamic_slice_in_dim(w_out, c * 512 + 256, 256, 0)
    half_a, half_b, q_up, q_down, wo_one, wo_two = lax.optimization_barrier(
        (half_a, half_b, q_up, q_down, wo_one, wo_two)
    )
    far_up = moved(q_up[:, 4 * QUART :], dz=1)
    far_down = moved(q_down[:, 4 * QUART :], dz=3)
    other_a = moved(half_a, dc=1)
    other_b = moved(half_b, dc=1)
    wo_m = [moved(wo_one, dx=1), moved(wo_two, dx=3)]
    wk_t, wv_t = moved(wk_m, dc=1), moved(wv_m, dc=1)
    low, high = select(sc, meta, half_a, other_a, half_b, other_b)
    low, high, far_up, far_down = lax.optimization_barrier((low, high, far_up, far_down))

    def spread(chosen):
        return moved(chosen, dz=1), moved(chosen, dz=3)

    def pass_on(back, ahead):
        return moved(back[:, :16], dz=1), moved(ahead[:, 16:], dz=3)

    def collect(chosen):
        back, ahead = spread(chosen)
        return (back, *pass_on(back, ahead), ahead)

    def nothing(chosen):
        none = jnp.zeros_like(chosen)
        return none, none[:, :16], none[:, :16], none

    back, ahead = spread(low)
    low = (low, back, *pass_on(back, ahead), ahead)
    *low, high, wk_t, wv_t, wo_m = lax.optimization_barrier((*low, high, wk_t, wv_t, wo_m))
    high = (high, *lax.cond(meta[0, 6] > FIRST, collect, nothing, high))
    *low, high, wo_m = lax.optimization_barrier((*low, high, wo_m))
    wo_t = [moved(w, dc=1) for w in wo_m]

    pieces = (*low, *high, *owns)
    w_parts = (w_out, *wo_m, *wo_t)
    wk, wv = (w_key, wk_m, wk_t), (w_value, wv_m, wv_t)
    heard = attend(0, sc, meta, (far_up, far_down, q_own), pieces, wk, wv)
    left, right, own = project(heard, w_parts)
    left, right, q_up = lax.optimization_barrier((left, right, q_up))
    above, below = moved(left, dz=1), moved(right, dz=3)
    heard = attend(1, sc, meta, (q_down, q_up, q_up), pieces, wk, wv)
    heard, above, below = lax.optimization_barrier((heard, above, below))
    up, down = project(heard, w_parts, (above, below))
    up, down = moved(up, dz=1), moved(down, dz=3)
    return (own.astype(F32) + up.astype(F32) + down.astype(F32)).astype(BF16)


def solution(mesh):
    in_specs = (
        P(("blk", "uly"), None),
        P(("blk", "uly"), None),
        P(),
        P(None, "uly"),
        P(None, "uly"),
        P("uly", None),
    )
    out_specs = P(("blk", "uly"), None)
    return jax.shard_map(local, mesh=mesh, in_specs=in_specs, out_specs=out_specs, check_vma=False)
```

```python
import math
from functools import partial

import numpy as np
import jax
import jax.numpy as jnp
from jax import lax
from jax.experimental import pallas as pl
from jax.experimental.pallas import tpu as pltpu
from jax.sharding import PartitionSpec as P

BLOCK = 128
NOPE = 128
ROPE = 64
VDIM = 128
LATENT = 512
WIDE = 640
SLOTS = 28
FIRST = 20
UNION = (8, 16, 8)
CALLS = ((2,), (1, 3), (0,))
QUART = 4 * (NOPE + ROPE)
COLS = 3584
F32 = jnp.float32
BF16 = jnp.bfloat16


def moved(value, dy=0, dx=0, dc=0, dz=0):
    pairs = []
    for y in range(4):
        for x in range(4):
            for c in range(2):
                for z in range(4):
                    place = lambda y, x, c, z: (y * 4 + (x // 2) * 2 + c) * 8 + (x % 2) * 4 + z
                    pairs.append(
                        (
                            place(y, x, c, z),
                            place((y + dy) % 4, (x + dx) % 4, (c + dc) % 2, (z + dz) % 4),
                        )
                    )
    return lax.ppermute(value, ("blk", "uly"), pairs)


def swap_halves(x):
    lane = lax.broadcasted_iota(jnp.int32, x.shape, 1)
    return jnp.where(lane % 64 < 32, pltpu.roll(x, 96, axis=1), pltpu.roll(x, 32, axis=1))


def prologue_kernel(sc, mask_ref, lat_ref, freq_ref, meta_ref, cos_ref, sin_ref, tmp):
    g, xl, z = sc[0], sc[1], sc[2]
    rows = mask_ref[pl.ds(pl.multiple_of(8 * g, 8), 8), :].astype(F32)
    ri = lax.broadcasted_iota(jnp.int32, (8, 128), 0)
    li = lax.broadcasted_iota(jnp.int32, (8, 128), 1)
    upper = (
        lax.broadcasted_iota(jnp.int32, (128, 128), 0) <= lax.broadcasted_iota(jnp.int32, (128, 128), 1)
    ).astype(F32)
    is_self = li == 8 * g + ri
    others = jnp.where(is_self, 0.0, rows)
    row_rank = jnp.dot(others, upper, preferred_element_type=F32)
    ahead = (ri + 8 - (xl * 4 + z)) % 4
    mine = ri // 4 == xl
    in_call = [mine & ((ahead == call[0]) | (ahead == call[-1])) for call in CALLS]

    def order(inside):
        wanted = jnp.broadcast_to(inside, (8, 128))
        return wanted, jnp.dot(wanted, upper, preferred_element_type=F32)

    calls = [order(jnp.max(jnp.where(rows_in, rows, 0.0), axis=0, keepdims=True)) for rows_in in in_call]
    own_at = li - (8 * g + 4 * xl)
    is_own = (own_at >= 0) & (own_at < 4)
    needed = jnp.max(jnp.where(mine & ~is_own, rows, 0.0), axis=0, keepdims=True)
    needed, order_all = order(needed)
    slot_of = jnp.where(is_own, own_at.astype(F32) + float(SLOTS), order_all - 1.0)
    place_of = jnp.where(in_call[0], calls[0][1], jnp.where(in_call[1], calls[1][1], calls[2][1])) - 1.0
    acc = jnp.where(li == 0, jnp.sum(jnp.where(is_self, place_of, 0.0), axis=1, keepdims=True), 0.0)
    for j in range(1, 8):
        hit = (row_rank == float(j)) & (others > 0.5)
        acc = jnp.where(li == j, jnp.sum(jnp.where(hit, place_of, 0.0), axis=1, keepdims=True), acc)
    depth = jnp.sum(rows, axis=1, keepdims=True)
    acc = jnp.where(li == 8, depth, acc)
    meta_ref[32:40, :] = acc.astype(jnp.int32)
    ci = lax.broadcasted_iota(jnp.int32, (32, 128), 0).astype(F32)
    cl = lax.broadcasted_iota(jnp.int32, (32, 128), 1)
    hit = (slot_of[0:1, :] == ci) & (needed[0:1, :] > 0.5)
    table = jnp.where(cl == 0, jnp.sum(jnp.where(hit, cl.astype(F32), 0.0), axis=1, keepdims=True), 0.0)
    for i, (inside, place) in enumerate(calls):
        hit = (place[0:1, :] == ci + 1.0) & (inside[0:1, :] > 0.5)
        slots = jnp.sum(jnp.where(hit, slot_of[0:1, :], 0.0), axis=1, keepdims=True)
        table = jnp.where(cl == 2 + i, slots, table)
        table = jnp.where(cl == 10 + i, jnp.max(place[0:1, :], axis=1, keepdims=True), table)
    group = lax.broadcasted_iota(jnp.int32, (128, 128), 0) // 4
    apart = group != lax.broadcasted_iota(jnp.int32, (128, 128), 1) // 4
    links = jnp.where(apart, mask_ref[...].astype(F32), 0.0)
    most = jnp.sum(jnp.max(links.reshape(32, 4, 128), axis=1), axis=1, keepdims=True)
    most = jnp.max(most, axis=0, keepdims=True)
    table = jnp.where(cl == 6, most, table)
    meta_ref[0:32, :] = table.astype(jnp.int32)

    own = jnp.sum(jnp.where(ri == xl * 4 + z, rows, 0.0), axis=1, keepdims=True)
    own = jnp.sum(own, axis=0, keepdims=True)
    token = lax.broadcasted_iota(jnp.int32, (128, 128), 0).astype(F32)
    angles = (128.0 * (own - 1.0) + token) * freq_ref[0:1, :]
    lane = lax.broadcasted_iota(jnp.int32, (128, 128), 1)
    cosine = jnp.cos(angles)
    sine = jnp.where(lane % 64 < 32, -jnp.sin(angles), jnp.sin(angles))
    cos_ref[...] = cosine
    sin_ref[...] = sine
    rope = lat_ref[:, LATENT:].astype(F32)
    rope = jnp.concatenate([rope, rope], axis=1)
    tmp[:, :LATENT] = lat_ref[:, :LATENT]
    tmp[:, LATENT:] = (rope * cosine + swap_halves(rope) * sine).astype(BF16)


def prologue(sc, block_mask, latents, freq):
    table = jax.ShapeDtypeStruct((128, 128), F32)
    return pl.pallas_call(
        prologue_kernel,
        grid_spec=pltpu.PrefetchScalarGridSpec(
            num_scalar_prefetch=1,
            grid=(),
            in_specs=[pl.BlockSpec(memory_space=pltpu.VMEM)] * 3,
            out_specs=[pl.BlockSpec(memory_space=pltpu.VMEM)] * 4,
        ),
        out_shape=[
            jax.ShapeDtypeStruct((40, 128), jnp.int32),
            table,
            table,
            jax.ShapeDtypeStruct((128, WIDE), BF16),
        ],
        name="prologue",
    )(sc, block_mask, latents, freq)


def query_kernel(sc, x0, x1, x3, cos_ref, sin_ref, own, up, down):
    step = pl.program_id(0)
    cosine, sine = cos_ref[...], sin_ref[...]
    lane = lax.broadcasted_iota(jnp.int32, (128, 128), 1)

    def prepare(x_ref, out):
        for pair in range(2):
            at = 384 * pair
            mid = x_ref[:, at + 128 : at + 256].astype(F32)
            last = x_ref[:, at + 256 : at + 384].astype(F32)
            second = pltpu.roll(jnp.where(lane < 64, last, mid), 64, axis=1)
            rope = jnp.where(lane < 64, mid, last)
            rope = rope * cosine + swap_halves(rope) * sine
            out[:, at : at + 128] = x_ref[:, at : at + 128]
            out[:, at + 128 : at + 256] = second.astype(BF16)
            out[:, at + 256 : at + 384] = rope.astype(BF16)

    @pl.when(step < 4)
    def _():
        prepare(x0, own)
        prepare(x1, up)
        prepare(x3, down)

    @pl.when(step >= 4)
    def _():
        prepare(x1, up)
        prepare(x3, down)


def query_prep(sc, queries, cosine, sine):
    def source(k):
        def index(t, sc):
            xl, z, c = sc[1], sc[2], sc[3]
            ahead, quarter = k, t
            if k in (1, 3):
                ahead = jnp.where(t < 4, k, 2)
                quarter = jnp.where(t < 4, t, t - 4 if k == 1 else t - 2)
            else:
                quarter = jnp.minimum(t, 3)
            zd = (z + ahead) % 4
            own = (xl * 4 + zd) * 2 + quarter
            other = ((1 - xl) * 4 + zd) * 2 + jnp.where(quarter == 2, c, 1 - c)
            return (0, jnp.where(quarter < 2, own, other))

        return pl.BlockSpec((128, QUART), index)

    table = pl.BlockSpec((128, 128), lambda t, sc: (0, 0))
    return pl.pallas_call(
        query_kernel,
        grid_spec=pltpu.PrefetchScalarGridSpec(
            num_scalar_prefetch=1,
            grid=(6,),
            in_specs=[source(k) for k in (0, 1, 3)] + [table, table],
            out_specs=[
                pl.BlockSpec((128, QUART), lambda t, sc: (0, jnp.minimum(t, 3))),
                pl.BlockSpec((128, QUART), lambda t, sc: (0, t)),
                pl.BlockSpec((128, QUART), lambda t, sc: (0, t)),
            ],
        ),
        out_shape=[jax.ShapeDtypeStruct((128, n * QUART), BF16) for n in (4, 6, 6)],
        name="query_prep",
    )(sc, queries, queries, queries, cosine, sine)


def select_kernel(sc, meta, a0, a1, b0, b1, low, high, sems):
    z, c, y, x = sc[2], sc[3], sc[4], sc[5]

    def copies(slot):
        block = meta[slot, 0]
        ze = (z + 4 - block % 4) % 4
        xl = (block // 4) % 2
        core = (block // 8) % 2
        xe = (x + 4 - ((block // 16) % 2 * 2 + xl)) % 4
        ye = (y + 4 - block // 32) % 4
        at_a = (ye * 4 + xe) * 4 + ze
        at_b = (xe * 4 + ye) * 4 + ze

        out, at = (low, slot) if slot < FIRST else (high, slot - FIRST)

        def pair(a, b):
            return [
                pltpu.make_async_copy(a.at[at_a], out.at[at, pl.ds(0, 16), :], sems.at[slot, 0]),
                pltpu.make_async_copy(b.at[at_b], out.at[at, pl.ds(16, 16), :], sems.at[slot, 1]),
            ]

        return core, pair

    for slot in range(SLOTS):
        core, pair = copies(slot)

        @pl.when(core == c)
        def _(pair=pair):
            for copy in pair(a0, b0):
                copy.start()

        @pl.when(core != c)
        def _(pair=pair):
            for copy in pair(a1, b1):
                copy.start()

    for slot in range(SLOTS):
        core, pair = copies(slot)
        for copy in pair(a0, b0):
            copy.wait()


def select(sc, meta, a0, a1, b0, b1):
    return pl.pallas_call(
        select_kernel,
        grid_spec=pltpu.PrefetchScalarGridSpec(
            num_scalar_prefetch=2,
            grid=(),
            in_specs=[pl.BlockSpec(memory_space=pl.ANY)] * 4,
            out_specs=[pl.BlockSpec(memory_space=pltpu.VMEM)] * 2,
            scratch_shapes=[pltpu.SemaphoreType.DMA((SLOTS, 2))],
        ),
        out_shape=[
            jax.ShapeDtypeStruct((FIRST, 32, WIDE), BF16),
            jax.ShapeDtypeStruct((SLOTS - FIRST, 32, WIDE), BF16),
        ],
        name="select_blocks",
    )(sc, meta, a0, a1, b0, b1)


def attend_kernel(which, sc, meta, *refs):
    n_q = 1 if which == 2 else 2
    q_refs, refs = refs[:n_q], refs[n_q:]
    low, high, owns, refs = refs[0:5], refs[5:10], refs[10:14], refs[14:]
    wks, wvs, heard = refs[0:3], refs[3:6], refs[6]
    rows_all, wk, wv, keys, vals, ropes, row_sems, w_sems = refs[7:]
    step = pl.program_id(0)
    xl, z = sc[1], sc[2]
    count = meta[0, 10 + which]

    def weight_copies(t):
        part = 0 if t < 2 else t - 1
        copies = []
        for i, (ws, w) in enumerate(((wks, wk), (wvs, wv))):
            source = ws[part]
            if t < 2:
                source = source.at[:, pl.ds(512 * t, 512)]
            copies.append(pltpu.make_async_copy(source, w.at[t], w_sems.at[t, i]))
        return copies

    def row_copies(u):
        slot = meta[u, 2 + which]
        ends = ((0, 32), (32, 32), (64, 16), (80, 16), (96, 32))

        def parts(sources, at):
            return [
                pltpu.make_async_copy(s.at[at], rows_all.at[u, pl.ds(first, n), :], row_sems.at[u, i])
                for i, (s, (first, n)) in enumerate(zip(sources, ends))
            ]

        def each(do):
            @pl.when(slot < FIRST)
            def _():
                for copy in parts(low, jnp.minimum(slot, FIRST - 1)):
                    do(copy)

            @pl.when((slot >= FIRST) & (slot < SLOTS))
            def _():
                for copy in parts(high, jnp.clip(slot - FIRST, 0, SLOTS - FIRST - 1)):
                    do(copy)

            for k, own_rows in enumerate(owns):

                @pl.when(slot == SLOTS + (z + 4 - k) % 4)
                def _(own_rows=own_rows):
                    do(pltpu.make_async_copy(own_rows, rows_all.at[u], row_sems.at[u, 0]))

        return each

    @pl.when(step == 0)
    def _():
        @pl.loop(0, count)
        def _(u):
            row_copies(u)(lambda copy: copy.start())

        for t in range(4):
            for copy in weight_copies(t):
                copy.start()

        @pl.loop(0, count)
        def _(u):
            row_copies(u)(lambda copy: copy.wait())
            ropes[u] = rows_all[u, :, LATENT:].T

    for t in range(4):

        @pl.when(step == t)
        def _(t=t):
            for copy in weight_copies(t):
                copy.wait()

    for chunk in range(UNION[which] // 4):

        @pl.when(chunk * 4 < count)
        def _(chunk=chunk):
            at = slice(chunk * 4, chunk * 4 + 4)
            latent = rows_all[at, :, :LATENT].reshape(512, LATENT)
            key = jnp.dot(latent, wk[step], preferred_element_type=F32).astype(BF16)
            for i in range(4):
                keys[chunk * 4 + i] = key[128 * i : 128 * i + 128].T
            vals[at] = jnp.dot(latent, wv[step], preferred_element_type=F32).astype(BF16).reshape(4, 128, 512)

    factor = math.log2(math.e) / math.sqrt(NOPE + ROPE)
    lane = lax.broadcasted_iota(jnp.int32, (128, 128), 1)
    row = lax.broadcasted_iota(jnp.int32, (128, 128), 0)
    causal = lane <= row

    for b in range(len(CALLS[which])):
        line = 32 + xl * 4 + (z + CALLS[which][b]) % 4
        depth = meta[line, 8]

        def run(tiles, b=b, line=line, depth=depth):
            def q_cols(first):
                part = q_refs[b][:, first : first + 128]
                if which == 0:
                    part = jnp.where(step < 2, part, q_refs[1][:, first : first + 128])
                return part

            at = [meta[line, j] for j in range(tiles)]
            for pair in range(2):
                first = 384 * pair
                both = slice(pair * 256, pair * 256 + 256)
                value = jnp.concatenate([vals[a, :, both] for a in at], axis=0)
                rope_all = q_cols(first + 256).astype(F32)
                probs, totals = [], []
                for half in range(2):
                    cols = slice(pair * 256 + half * 128, pair * 256 + half * 128 + 128)
                    mine = (lane < 64) if half == 0 else (lane >= 64)
                    rope = jnp.where(mine, rope_all, 0.0)
                    query = jnp.concatenate([q_cols(first + 128 * half), rope.astype(BF16)], axis=1)
                    key = jnp.concatenate(
                        [jnp.concatenate([keys[a, cols, :], ropes[a]], axis=0) for a in at],
                        axis=1,
                    )
                    scores = jnp.dot(query, key, preferred_element_type=F32)
                    scores = [scores[:, 128 * j : 128 * j + 128] for j in range(tiles)]
                    scores[0] = jnp.where(causal, scores[0], -jnp.inf)
                    scores[-1] = jnp.where(tiles - 1 < depth, scores[-1], -jnp.inf)
                    peak = scores[0]
                    for s in scores[1:]:
                        peak = jnp.maximum(peak, s)
                    peak = jnp.max(peak, axis=1, keepdims=True)
                    weights = [jnp.exp2((s - peak) * factor) for s in scores]
                    total = weights[0]
                    for w in weights[1:]:
                        total = total + w
                    totals.append(jnp.sum(total, axis=1, keepdims=True))
                    probs.append(jnp.concatenate([w.astype(BF16) for w in weights], axis=1))
                found = jnp.dot(jnp.concatenate(probs, axis=0), value, preferred_element_type=F32)
                for half in range(2):
                    cols = slice(pair * 256 + half * 128, pair * 256 + half * 128 + 128)
                    part = found[half * 128 : half * 128 + 128, half * 128 : half * 128 + 128]
                    heard[b * 128 : b * 128 + 128, cols] = (part / totals[half]).astype(BF16)

        for tiles in (2, 4, 6, 8):

            @pl.when((depth == tiles) | (depth == tiles - 1))
            def _(run=run, tiles=tiles):
                run(tiles)


def attend(which, sc, meta, queries, pieces, wk, wv):
    rows = 128 * len(CALLS[which])
    union = UNION[which]
    q_specs = [pl.BlockSpec((128, QUART), lambda t, sc, m: (0, t)) for q in queries]
    if which == 0:
        q_specs = [
            pl.BlockSpec((128, QUART), lambda t, sc, m: (0, jnp.minimum(t, 1))),
            pl.BlockSpec((128, QUART), lambda t, sc, m: (0, jnp.maximum(t - 2, 0))),
        ]
    hbm = pl.BlockSpec(memory_space=pltpu.HBM)
    return pl.pallas_call(
        partial(attend_kernel, which),
        grid_spec=pltpu.PrefetchScalarGridSpec(
            num_scalar_prefetch=2,
            grid=(4,),
            in_specs=q_specs + [hbm] * (len(pieces) + 6),
            out_specs=pl.BlockSpec((rows, 512), lambda t, sc, m: (0, t)),
            scratch_shapes=[
                pltpu.VMEM((union, 128, WIDE), BF16),
                pltpu.VMEM((4, LATENT, 512), BF16),
                pltpu.VMEM((4, LATENT, 512), BF16),
                pltpu.VMEM((union, 512, 128), BF16),
                pltpu.VMEM((union, 128, 512), BF16),
                pltpu.VMEM((union, 128, 128), BF16),
                pltpu.SemaphoreType.DMA((union, 5)),
                pltpu.SemaphoreType.DMA((4, 2)),
            ],
        ),
        out_shape=pltpu.HBM((rows, 2048), BF16),
        compiler_params=pltpu.CompilerParams(vmem_limit_bytes=40 * 2**20),
        name="attend_%d" % which,
    )(sc, meta, *[pltpu.with_memory_space_constraint(a, pltpu.HBM) for a in (*queries, *pieces, *wk, *wv)])


def project_kernel(which, heard, *refs):
    ws, refs = refs[:5], refs[5:]
    step = pl.program_id(0)
    w = jnp.concatenate([w[...] for w in ws], axis=0)
    total = jnp.dot(heard[...], w, preferred_element_type=F32)
    if which == 0:
        left, right = refs

        @pl.when(step < 2)
        def _():
            left[...] = total.astype(BF16)

        @pl.when(step >= 2)
        def _():
            right[...] = total.astype(BF16)

    elif which == 1:
        above, below, up, down = refs
        up[...] = (total[:128] + jnp.where(step < 2, above[...].astype(F32), 0.0)).astype(BF16)
        down[...] = (total[128:] + jnp.where(step < 2, 0.0, below[...].astype(F32))).astype(BF16)
    else:
        up, down, out = refs
        out[...] = (total + up[...].astype(F32) + down[...].astype(F32)).astype(BF16)


def project(which, heard, w_parts, received=()):
    cols = COLS // 4
    each = pl.BlockSpec((128, cols), lambda n: (0, n))
    left = pl.BlockSpec((128, cols), lambda n: (0, jnp.minimum(n, 1)))
    right = pl.BlockSpec((128, cols), lambda n: (0, jnp.maximum(n - 2, 0)))
    whole = jax.ShapeDtypeStruct((128, COLS), BF16)
    half = jax.ShapeDtypeStruct((128, COLS // 2), BF16)
    return pl.pallas_call(
        partial(project_kernel, which),
        grid=(4,),
        in_specs=[pl.BlockSpec(heard.shape, lambda n: (0, 0))]
        + [pl.BlockSpec((w.shape[0], cols), lambda n: (0, n)) for w in w_parts]
        + [[], [left, right], [each, each]][which],
        out_specs=[[left, right], [each, each], each][which],
        out_shape=[[half, half], [whole, whole], whole][which],
        compiler_params=pltpu.CompilerParams(vmem_limit_bytes=32 * 2**20),
        name="project",
    )(pltpu.with_memory_space_constraint(heard, pltpu.HBM), *w_parts, *received)


def gather_ring(value, axis):
    one = moved(value, **{axis: 1})
    three = moved(value, **{axis: 3})
    two = moved(value, **{axis: 2})
    return jnp.concatenate([value, one, two, three], axis=0)


def local(queries, latents, block_mask, w_key, w_value, w_out):
    g = lax.axis_index("blk").astype(jnp.int32)
    u = lax.axis_index("uly").astype(jnp.int32)
    c, y, xl, z = g % 2, g // 4, u // 4, u % 4
    x = (g // 2) % 2 * 2 + xl
    sc = jnp.stack([g, xl, z, c, y, x])
    freq = np.float32(10000.0) ** (-np.arange(32, dtype=np.float32) / np.float32(32))
    freq = jnp.asarray(np.tile(freq[None, :], (8, 4)))

    meta, cosine, sine, block = prologue(sc, block_mask, latents, freq)
    owns = [block, moved(block, dz=1), moved(block, dz=2), moved(block, dz=3)]
    q_own, q_up, q_down = query_prep(sc, queries, cosine, sine)
    mine = jnp.stack([lax.dynamic_slice_in_dim(own, 32 * z, 32, 0) for own in owns])
    half_a, half_b = mine[:, :16], mine[:, 16:]
    wk_m = moved(lax.dynamic_slice_in_dim(w_key, c * 512, 512, 1), dx=1)
    wv_m = moved(lax.dynamic_slice_in_dim(w_value, c * 512, 512, 1), dx=3)
    half_a, half_b, q_up, q_down, wk_m, wv_m = lax.optimization_barrier(
        (half_a, half_b, q_up, q_down, wk_m, wv_m)
    )

    q_up, q_down = moved(q_up, dz=1), moved(q_down, dz=3)
    half_a = gather_ring(half_a, "dx")
    half_b = gather_ring(half_b, "dy")

    half_a, half_b = lax.optimization_barrier((half_a, half_b))
    half_a = gather_ring(half_a, "dy")
    half_b = gather_ring(half_b, "dx")
    wo_one = lax.dynamic_slice_in_dim(w_out, c * 512, 256, 0)
    wo_two = lax.dynamic_slice_in_dim(w_out, c * 512 + 256, 256, 0)
    half_a, half_b, q_up, q_down, wo_one, wo_two = lax.optimization_barrier(
        (half_a, half_b, q_up, q_down, wo_one, wo_two)
    )
    far_up = moved(q_up[:, 4 * QUART :], dz=1)
    far_down = moved(q_down[:, 4 * QUART :], dz=3)
    other_a = moved(half_a, dc=1)
    other_b = moved(half_b, dc=1)
    wo_m = [moved(wo_one, dx=1), moved(wo_two, dx=3)]
    wk_t, wv_t = moved(wk_m, dc=1), moved(wv_m, dc=1)
    low, high = select(sc, meta, half_a, other_a, half_b, other_b)
    low, high, far_up, far_down = lax.optimization_barrier((low, high, far_up, far_down))

    def spread(chosen):
        return moved(chosen, dz=1), moved(chosen, dz=3)

    def pass_on(back, ahead):
        return moved(back[:, :16], dz=1), moved(ahead[:, 16:], dz=3)

    def collect(chosen):
        back, ahead = spread(chosen)
        return (back, *pass_on(back, ahead), ahead)

    def nothing(chosen):
        none = jnp.zeros_like(chosen)
        return none, none[:, :16], none[:, :16], none

    back, ahead = spread(low)
    low = (low, back, *pass_on(back, ahead), ahead)
    *low, high, wk_t, wv_t, wo_m = lax.optimization_barrier((*low, high, wk_t, wv_t, wo_m))
    high = (high, *lax.cond(meta[0, 6] > FIRST, collect, nothing, high))
    *low, high, wo_m = lax.optimization_barrier((*low, high, wo_m))
    wo_t = [moved(w, dc=1) for w in wo_m]

    pieces = (*low, *high, *owns)
    w_parts = (w_out, *wo_m, *wo_t)
    wk, wv = (w_key, wk_m, wk_t), (w_value, wv_m, wv_t)
    heard = attend(0, sc, meta, (far_up, far_down), pieces, wk, wv)
    left, right = project(0, heard, w_parts)
    left, right, q_up = lax.optimization_barrier((left, right, q_up))
    above, below = moved(left, dz=1), moved(right, dz=3)
    heard = attend(1, sc, meta, (q_down, q_up), pieces, wk, wv)
    heard, above, below = lax.optimization_barrier((heard, above, below))
    up, down = project(1, heard, w_parts, (above, below))
    up, down, q_own = lax.optimization_barrier((up, down, q_own))
    up, down = moved(up, dz=1), moved(down, dz=3)
    heard = attend(2, sc, meta, (q_own,), pieces, wk, wv)
    heard, up, down = lax.optimization_barrier((heard, up, down))
    return project(2, heard, w_parts, (up, down))


def solution(mesh):
    in_specs = (
        P(("blk", "uly"), None),
        P(("blk", "uly"), None),
        P(),
        P(None, "uly"),
        P(None, "uly"),
        P("uly", None),
    )
    out_specs = P(("blk", "uly"), None)
    return jax.shard_map(local, mesh=mesh, in_specs=in_specs, out_specs=out_specs, check_vma=False)
```

```python
import math
from functools import partial

import numpy as np
import jax
import jax.numpy as jnp
from jax import lax
from jax.experimental import pallas as pl
from jax.experimental.pallas import tpu as pltpu
from jax.sharding import PartitionSpec as P

BLOCK = 128
NOPE = 128
ROPE = 64
VDIM = 128
LATENT = 512
WIDE = 640
SLOTS = 28
FIRST = 20
UNION = (8, 16, 8)
CALLS = ((2,), (1, 3), (0,))
QUART = 4 * (NOPE + ROPE)
COLS = 3584
F32 = jnp.float32
BF16 = jnp.bfloat16


def moved(value, dy=0, dx=0, dc=0, dz=0):
    pairs = []
    for y in range(4):
        for x in range(4):
            for c in range(2):
                for z in range(4):
                    place = lambda y, x, c, z: (y * 4 + (x // 2) * 2 + c) * 8 + (x % 2) * 4 + z
                    pairs.append(
                        (
                            place(y, x, c, z),
                            place((y + dy) % 4, (x + dx) % 4, (c + dc) % 2, (z + dz) % 4),
                        )
                    )
    return lax.ppermute(value, ("blk", "uly"), pairs)


def swap_halves(x):
    lane = lax.broadcasted_iota(jnp.int32, x.shape, 1)
    return jnp.where(lane % 64 < 32, pltpu.roll(x, 96, axis=1), pltpu.roll(x, 32, axis=1))


def prologue_kernel(sc, mask_ref, lat_ref, freq_ref, meta_ref, cos_ref, sin_ref, tmp):
    g, xl, z = sc[0], sc[1], sc[2]
    rows = mask_ref[pl.ds(pl.multiple_of(8 * g, 8), 8), :].astype(F32)
    ri = lax.broadcasted_iota(jnp.int32, (8, 128), 0)
    li = lax.broadcasted_iota(jnp.int32, (8, 128), 1)
    upper = (
        lax.broadcasted_iota(jnp.int32, (128, 128), 0) <= lax.broadcasted_iota(jnp.int32, (128, 128), 1)
    ).astype(F32)
    is_self = li == 8 * g + ri
    others = jnp.where(is_self, 0.0, rows)
    row_rank = jnp.dot(others, upper, preferred_element_type=F32)
    ahead = (ri + 8 - (xl * 4 + z)) % 4
    mine = ri // 4 == xl
    in_call = [mine & ((ahead == call[0]) | (ahead == call[-1])) for call in CALLS]

    def order(inside):
        wanted = jnp.broadcast_to(inside, (8, 128))
        return wanted, jnp.dot(wanted, upper, preferred_element_type=F32)

    calls = [order(jnp.max(jnp.where(rows_in, rows, 0.0), axis=0, keepdims=True)) for rows_in in in_call]
    own_at = li - (8 * g + 4 * xl)
    is_own = (own_at >= 0) & (own_at < 4)
    needed = jnp.max(jnp.where(mine & ~is_own, rows, 0.0), axis=0, keepdims=True)
    needed, order_all = order(needed)
    slot_of = jnp.where(is_own, own_at.astype(F32) + float(SLOTS), order_all - 1.0)
    place_of = jnp.where(in_call[0], calls[0][1], jnp.where(in_call[1], calls[1][1], calls[2][1])) - 1.0
    acc = jnp.where(li == 0, jnp.sum(jnp.where(is_self, place_of, 0.0), axis=1, keepdims=True), 0.0)
    for j in range(1, 8):
        hit = (row_rank == float(j)) & (others > 0.5)
        acc = jnp.where(li == j, jnp.sum(jnp.where(hit, place_of, 0.0), axis=1, keepdims=True), acc)
    depth = jnp.sum(rows, axis=1, keepdims=True)
    acc = jnp.where(li == 8, depth, acc)
    meta_ref[32:40, :] = acc.astype(jnp.int32)
    ci = lax.broadcasted_iota(jnp.int32, (32, 128), 0).astype(F32)
    cl = lax.broadcasted_iota(jnp.int32, (32, 128), 1)
    hit = (slot_of[0:1, :] == ci) & (needed[0:1, :] > 0.5)
    table = jnp.where(cl == 0, jnp.sum(jnp.where(hit, cl.astype(F32), 0.0), axis=1, keepdims=True), 0.0)
    for i, (inside, place) in enumerate(calls):
        hit = (place[0:1, :] == ci + 1.0) & (inside[0:1, :] > 0.5)
        slots = jnp.sum(jnp.where(hit, slot_of[0:1, :], 0.0), axis=1, keepdims=True)
        table = jnp.where(cl == 2 + i, slots, table)
        table = jnp.where(cl == 10 + i, jnp.max(place[0:1, :], axis=1, keepdims=True), table)
    group = lax.broadcasted_iota(jnp.int32, (128, 128), 0) // 4
    apart = group != lax.broadcasted_iota(jnp.int32, (128, 128), 1) // 4
    links = jnp.where(apart, mask_ref[...].astype(F32), 0.0)
    most = jnp.sum(jnp.max(links.reshape(32, 4, 128), axis=1), axis=1, keepdims=True)
    most = jnp.max(most, axis=0, keepdims=True)
    table = jnp.where(cl == 6, most, table)
    meta_ref[0:32, :] = table.astype(jnp.int32)

    own = jnp.sum(jnp.where(ri == xl * 4 + z, rows, 0.0), axis=1, keepdims=True)
    own = jnp.sum(own, axis=0, keepdims=True)
    token = lax.broadcasted_iota(jnp.int32, (128, 128), 0).astype(F32)
    angles = (128.0 * (own - 1.0) + token) * freq_ref[0:1, :]
    lane = lax.broadcasted_iota(jnp.int32, (128, 128), 1)
    cosine = jnp.cos(angles)
    sine = jnp.where(lane % 64 < 32, -jnp.sin(angles), jnp.sin(angles))
    cos_ref[...] = cosine
    sin_ref[...] = sine
    rope = lat_ref[:, LATENT:].astype(F32)
    rope = jnp.concatenate([rope, rope], axis=1)
    tmp[:, :LATENT] = lat_ref[:, :LATENT]
    tmp[:, LATENT:] = (rope * cosine + swap_halves(rope) * sine).astype(BF16)


def prologue(sc, block_mask, latents, freq):
    table = jax.ShapeDtypeStruct((128, 128), F32)
    return pl.pallas_call(
        prologue_kernel,
        grid_spec=pltpu.PrefetchScalarGridSpec(
            num_scalar_prefetch=1,
            grid=(),
            in_specs=[pl.BlockSpec(memory_space=pltpu.VMEM)] * 3,
            out_specs=[pl.BlockSpec(memory_space=pltpu.VMEM)] * 4,
        ),
        out_shape=[
            jax.ShapeDtypeStruct((40, 128), jnp.int32),
            table,
            table,
            jax.ShapeDtypeStruct((128, WIDE), BF16),
        ],
        name="prologue",
    )(sc, block_mask, latents, freq)


def query_kernel(sc, x0, x1, x3, cos_ref, sin_ref, own, up, down):
    step = pl.program_id(0)
    cosine, sine = cos_ref[...], sin_ref[...]
    lane = lax.broadcasted_iota(jnp.int32, (128, 128), 1)

    def prepare(x_ref, out):
        for pair in range(2):
            at = 384 * pair
            mid = x_ref[:, at + 128 : at + 256].astype(F32)
            last = x_ref[:, at + 256 : at + 384].astype(F32)
            second = pltpu.roll(jnp.where(lane < 64, last, mid), 64, axis=1)
            rope = jnp.where(lane < 64, mid, last)
            rope = rope * cosine + swap_halves(rope) * sine
            out[:, at : at + 128] = x_ref[:, at : at + 128]
            out[:, at + 128 : at + 256] = second.astype(BF16)
            out[:, at + 256 : at + 384] = rope.astype(BF16)

    @pl.when(step < 4)
    def _():
        prepare(x0, own)
        prepare(x1, up)
        prepare(x3, down)

    @pl.when(step >= 4)
    def _():
        prepare(x1, up)
        prepare(x3, down)


def query_prep(sc, queries, cosine, sine):
    def source(k):
        def index(t, sc):
            xl, z, c = sc[1], sc[2], sc[3]
            ahead, quarter = k, t
            if k in (1, 3):
                ahead = jnp.where(t < 4, k, 2)
                quarter = jnp.where(t < 4, t, t - 4 if k == 1 else t - 2)
            else:
                quarter = jnp.minimum(t, 3)
            zd = (z + ahead) % 4
            own = (xl * 4 + zd) * 2 + quarter
            other = ((1 - xl) * 4 + zd) * 2 + jnp.where(quarter == 2, c, 1 - c)
            return (0, jnp.where(quarter < 2, own, other))

        return pl.BlockSpec((128, QUART), index)

    table = pl.BlockSpec((128, 128), lambda t, sc: (0, 0))
    return pl.pallas_call(
        query_kernel,
        grid_spec=pltpu.PrefetchScalarGridSpec(
            num_scalar_prefetch=1,
            grid=(6,),
            in_specs=[source(k) for k in (0, 1, 3)] + [table, table],
            out_specs=[
                pl.BlockSpec((None, 128, QUART), lambda t, sc: (jnp.minimum(t, 3), 0, 0)),
                pl.BlockSpec((None, 128, QUART), lambda t, sc: (t, 0, 0)),
                pl.BlockSpec((None, 128, QUART), lambda t, sc: (t, 0, 0)),
            ],
        ),
        out_shape=[jax.ShapeDtypeStruct((n, 128, QUART), BF16) for n in (4, 6, 6)],
        name="query_prep",
    )(sc, queries, queries, queries, cosine, sine)


def select_kernel(sc, meta, a0, a1, b0, b1, low, high, sems):
    z, c, y, x = sc[2], sc[3], sc[4], sc[5]

    def copies(slot):
        block = meta[slot, 0]
        ze = (z + 4 - block % 4) % 4
        xl = (block // 4) % 2
        core = (block // 8) % 2
        xe = (x + 4 - ((block // 16) % 2 * 2 + xl)) % 4
        ye = (y + 4 - block // 32) % 4
        at_a = (ye * 4 + xe) * 4 + ze
        at_b = (xe * 4 + ye) * 4 + ze

        out, at = (low, slot) if slot < FIRST else (high, slot - FIRST)

        def pair(a, b):
            return [
                pltpu.make_async_copy(a.at[at_a], out.at[at, pl.ds(0, 16), :], sems.at[slot, 0]),
                pltpu.make_async_copy(b.at[at_b], out.at[at, pl.ds(16, 16), :], sems.at[slot, 1]),
            ]

        return core, pair

    for slot in range(SLOTS):
        core, pair = copies(slot)

        @pl.when(core == c)
        def _(pair=pair):
            for copy in pair(a0, b0):
                copy.start()

        @pl.when(core != c)
        def _(pair=pair):
            for copy in pair(a1, b1):
                copy.start()

    for slot in range(SLOTS):
        core, pair = copies(slot)
        for copy in pair(a0, b0):
            copy.wait()


def select(sc, meta, a0, a1, b0, b1):
    return pl.pallas_call(
        select_kernel,
        grid_spec=pltpu.PrefetchScalarGridSpec(
            num_scalar_prefetch=2,
            grid=(),
            in_specs=[pl.BlockSpec(memory_space=pl.ANY)] * 4,
            out_specs=[pl.BlockSpec(memory_space=pltpu.VMEM)] * 2,
            scratch_shapes=[pltpu.SemaphoreType.DMA((SLOTS, 2))],
        ),
        out_shape=[
            jax.ShapeDtypeStruct((FIRST, 32, WIDE), BF16),
            jax.ShapeDtypeStruct((SLOTS - FIRST, 32, WIDE), BF16),
        ],
        name="select_blocks",
    )(sc, meta, a0, a1, b0, b1)


def attend_kernel(which, sc, meta, *refs):
    n_q = 1 if which == 2 else 2
    q_refs, refs = refs[:n_q], refs[n_q:]
    low, high, owns, refs = refs[0:5], refs[5:7], refs[7:11], refs[11:]
    wks, wvs, heard = refs[0:3], refs[3:6], refs[6]
    rows_all, wk, wv, keys, vals, ropes, row_sems, w_sems = refs[7:]
    step = pl.program_id(0)
    xl, z = sc[1], sc[2]
    count = meta[0, 10 + which]

    def weight_copies(t):
        part = 0 if t < 2 else t - 1
        copies = []
        for i, (ws, w) in enumerate(((wks, wk), (wvs, wv))):
            source = ws[part]
            if t < 2:
                source = source.at[:, pl.ds(512 * t, 512)]
            copies.append(pltpu.make_async_copy(source, w.at[t], w_sems.at[t, i]))
        return copies

    def row_copies(u):
        slot = meta[u, 2 + which]

        def parts(sources):
            ends = ((0, 32), (32, 96)) if len(sources) == 2 else ((0, 32), (32, 32), (64, 16), (80, 16), (96, 32))
            return [
                pltpu.make_async_copy(source, rows_all.at[u, pl.ds(first, n), :], row_sems.at[u, i])
                for i, (source, (first, n)) in enumerate(zip(sources, ends))
            ]

        def each(do):
            @pl.when(slot < FIRST)
            def _():
                at = jnp.minimum(slot, FIRST - 1)
                for copy in parts([piece.at[at] for piece in low]):
                    do(copy)

            @pl.when((slot >= FIRST) & (slot < SLOTS))
            def _():
                at = jnp.clip(slot - FIRST, 0, SLOTS - FIRST - 1)
                for copy in parts([high[0].at[at], high[1].at[at]]):
                    do(copy)

            for k, own_rows in enumerate(owns):

                @pl.when(slot == SLOTS + (z + 4 - k) % 4)
                def _(own_rows=own_rows):
                    do(pltpu.make_async_copy(own_rows, rows_all.at[u], row_sems.at[u, 0]))

        return each

    @pl.when(step == 0)
    def _():
        @pl.loop(0, count)
        def _(u):
            row_copies(u)(lambda copy: copy.start())

        for t in range(4):
            for copy in weight_copies(t):
                copy.start()

        @pl.loop(0, count)
        def _(u):
            row_copies(u)(lambda copy: copy.wait())
            ropes[u] = rows_all[u, :, LATENT:].T

    for t in range(4):

        @pl.when(step == t)
        def _(t=t):
            for copy in weight_copies(t):
                copy.wait()

    for chunk in range(UNION[which] // 4):

        @pl.when(chunk * 4 < count)
        def _(chunk=chunk):
            at = slice(chunk * 4, chunk * 4 + 4)
            latent = rows_all[at, :, :LATENT].reshape(512, LATENT)
            key = jnp.dot(latent, wk[step], preferred_element_type=F32).astype(BF16)
            for i in range(4):
                keys[chunk * 4 + i] = key[128 * i : 128 * i + 128].T
            vals[at] = jnp.dot(latent, wv[step], preferred_element_type=F32).astype(BF16).reshape(4, 128, 512)

    factor = math.log2(math.e) / math.sqrt(NOPE + ROPE)
    lane = lax.broadcasted_iota(jnp.int32, (128, 128), 1)
    row = lax.broadcasted_iota(jnp.int32, (128, 128), 0)
    causal = lane <= row

    for b in range(len(CALLS[which])):
        line = 32 + xl * 4 + (z + CALLS[which][b]) % 4
        depth = meta[line, 8]

        def run(tiles, b=b, line=line, depth=depth):
            def q_cols(first):
                part = q_refs[b][:, first : first + 128]
                if which == 0:
                    part = jnp.where(step < 2, part, q_refs[1][:, first : first + 128])
                return part

            at = [meta[line, j] for j in range(tiles)]
            for pair in range(2):
                first = 384 * pair
                both = slice(pair * 256, pair * 256 + 256)
                value = jnp.concatenate([vals[a, :, both] for a in at], axis=0)
                rope_all = q_cols(first + 256).astype(F32)
                probs, totals = [], []
                for half in range(2):
                    cols = slice(pair * 256 + half * 128, pair * 256 + half * 128 + 128)
                    mine = (lane < 64) if half == 0 else (lane >= 64)
                    rope = jnp.where(mine, rope_all, 0.0)
                    query = jnp.concatenate([q_cols(first + 128 * half), rope.astype(BF16)], axis=1)
                    key = jnp.concatenate(
                        [jnp.concatenate([keys[a, cols, :], ropes[a]], axis=0) for a in at],
                        axis=1,
                    )
                    scores = jnp.dot(query, key, preferred_element_type=F32)
                    scores = [scores[:, 128 * j : 128 * j + 128] for j in range(tiles)]
                    scores[0] = jnp.where(causal, scores[0], -jnp.inf)
                    scores[-1] = jnp.where(tiles - 1 < depth, scores[-1], -jnp.inf)
                    peak = scores[0]
                    for s in scores[1:]:
                        peak = jnp.maximum(peak, s)
                    peak = jnp.max(peak, axis=1, keepdims=True)
                    weights = [jnp.exp2((s - peak) * factor) for s in scores]
                    total = weights[0]
                    for w in weights[1:]:
                        total = total + w
                    totals.append(jnp.sum(total, axis=1, keepdims=True))
                    probs.append(jnp.concatenate([w.astype(BF16) for w in weights], axis=1))
                found = jnp.dot(jnp.concatenate(probs, axis=0), value, preferred_element_type=F32)
                for half in range(2):
                    cols = slice(pair * 256 + half * 128, pair * 256 + half * 128 + 128)
                    part = found[half * 128 : half * 128 + 128, half * 128 : half * 128 + 128]
                    heard[b * 128 : b * 128 + 128, cols] = (part / totals[half]).astype(BF16)

        for tiles in (2, 4, 6, 8):

            @pl.when((depth == tiles) | (depth == tiles - 1))
            def _(run=run, tiles=tiles):
                run(tiles)


def attend(which, sc, meta, queries, pieces, wk, wv):
    rows = 128 * len(CALLS[which])
    union = UNION[which]
    q_specs = [pl.BlockSpec((None, 128, QUART), lambda t, sc, m: (t, 0, 0)) for q in queries]
    if which == 0:
        q_specs = [
            pl.BlockSpec((None, 128, QUART), lambda t, sc, m: (jnp.minimum(t, 1), 0, 0)),
            pl.BlockSpec((None, 128, QUART), lambda t, sc, m: (jnp.maximum(t - 2, 0), 0, 0)),
        ]
    hbm = pl.BlockSpec(memory_space=pltpu.HBM)
    return pl.pallas_call(
        partial(attend_kernel, which),
        grid_spec=pltpu.PrefetchScalarGridSpec(
            num_scalar_prefetch=2,
            grid=(4,),
            in_specs=q_specs + [hbm] * (len(pieces) + 6),
            out_specs=pl.BlockSpec((rows, 512), lambda t, sc, m: (0, t)),
            scratch_shapes=[
                pltpu.VMEM((union, 128, WIDE), BF16),
                pltpu.VMEM((4, LATENT, 512), BF16),
                pltpu.VMEM((4, LATENT, 512), BF16),
                pltpu.VMEM((union, 512, 128), BF16),
                pltpu.VMEM((union, 128, 512), BF16),
                pltpu.VMEM((union, 128, 128), BF16),
                pltpu.SemaphoreType.DMA((union, 5)),
                pltpu.SemaphoreType.DMA((4, 2)),
            ],
        ),
        out_shape=pltpu.HBM((rows, 2048), BF16),
        compiler_params=pltpu.CompilerParams(vmem_limit_bytes=40 * 2**20),
        name="attend_%d" % which,
    )(sc, meta, *[pltpu.with_memory_space_constraint(a, pltpu.HBM) for a in (*queries, *pieces, *wk, *wv)])


def project_kernel(which, heard, *refs):
    ws, refs = refs[:5], refs[5:]
    step = pl.program_id(0)
    w = jnp.concatenate([w[...] for w in ws], axis=0)
    total = jnp.dot(heard[...], w, preferred_element_type=F32)
    if which == 0:
        left, right = refs

        @pl.when(step < 2)
        def _():
            left[...] = total.astype(BF16)

        @pl.when(step >= 2)
        def _():
            right[...] = total.astype(BF16)

    elif which == 1:
        above, below, up, down = refs
        up[...] = (total[:128] + jnp.where(step < 2, above[...].astype(F32), 0.0)).astype(BF16)
        down[...] = (total[128:] + jnp.where(step < 2, 0.0, below[...].astype(F32))).astype(BF16)
    else:
        up, down, out = refs
        out[...] = (total + up[...].astype(F32) + down[...].astype(F32)).astype(BF16)


def project(which, heard, w_parts, received=()):
    cols = COLS // 4
    each = pl.BlockSpec((128, cols), lambda n: (0, n))
    left = pl.BlockSpec((128, cols), lambda n: (0, jnp.minimum(n, 1)))
    right = pl.BlockSpec((128, cols), lambda n: (0, jnp.maximum(n - 2, 0)))
    whole = jax.ShapeDtypeStruct((128, COLS), BF16)
    half = jax.ShapeDtypeStruct((128, COLS // 2), BF16)
    return pl.pallas_call(
        partial(project_kernel, which),
        grid=(4,),
        in_specs=[pl.BlockSpec(heard.shape, lambda n: (0, 0))]
        + [pl.BlockSpec((w.shape[0], cols), lambda n: (0, n)) for w in w_parts]
        + [[], [left, right], [each, each]][which],
        out_specs=[[left, right], [each, each], each][which],
        out_shape=[[half, half], [whole, whole], whole][which],
        compiler_params=pltpu.CompilerParams(vmem_limit_bytes=32 * 2**20),
        name="project",
    )(pltpu.with_memory_space_constraint(heard, pltpu.HBM), *w_parts, *received)


def gather_ring(value, axis):
    one = moved(value, **{axis: 1})
    three = moved(value, **{axis: 3})
    two = moved(value, **{axis: 2})
    return jnp.concatenate([value, one, two, three], axis=0)


def local(queries, latents, block_mask, w_key, w_value, w_out):
    g = lax.axis_index("blk").astype(jnp.int32)
    u = lax.axis_index("uly").astype(jnp.int32)
    c, y, xl, z = g % 2, g // 4, u // 4, u % 4
    x = (g // 2) % 2 * 2 + xl
    sc = jnp.stack([g, xl, z, c, y, x])
    freq = np.float32(10000.0) ** (-np.arange(32, dtype=np.float32) / np.float32(32))
    freq = jnp.asarray(np.tile(freq[None, :], (8, 4)))

    meta, cosine, sine, block = prologue(sc, block_mask, latents, freq)
    owns = [block, moved(block, dz=1), moved(block, dz=2), moved(block, dz=3)]
    q_own, q_up, q_down = query_prep(sc, queries, cosine, sine)
    mine = jnp.stack([lax.dynamic_slice_in_dim(own, 32 * z, 32, 0) for own in owns])
    half_a, half_b = mine[:, :16], mine[:, 16:]
    wk_m = moved(lax.dynamic_slice_in_dim(w_key, c * 512, 512, 1), dx=1)
    wv_m = moved(lax.dynamic_slice_in_dim(w_value, c * 512, 512, 1), dx=3)
    half_a, half_b, q_up, q_down, wk_m, wv_m = lax.optimization_barrier(
        (half_a, half_b, q_up, q_down, wk_m, wv_m)
    )

    q_up, q_down = moved(q_up, dz=1), moved(q_down, dz=3)
    half_a = gather_ring(half_a, "dx")
    half_b = gather_ring(half_b, "dy")

    half_a, half_b = lax.optimization_barrier((half_a, half_b))
    half_a = gather_ring(half_a, "dy")
    half_b = gather_ring(half_b, "dx")
    wo_one = lax.dynamic_slice_in_dim(w_out, c * 512, 256, 0)
    wo_two = lax.dynamic_slice_in_dim(w_out, c * 512 + 256, 256, 0)
    half_a, half_b, q_up, q_down, wo_one, wo_two = lax.optimization_barrier(
        (half_a, half_b, q_up, q_down, wo_one, wo_two)
    )
    far_up = moved(q_up[4:], dz=1)
    far_down = moved(q_down[4:], dz=3)
    other_a = moved(half_a, dc=1)
    other_b = moved(half_b, dc=1)
    wo_m = [moved(wo_one, dx=1), moved(wo_two, dx=3)]
    wk_t, wv_t = moved(wk_m, dc=1), moved(wv_m, dc=1)
    low, high = select(sc, meta, half_a, other_a, half_b, other_b)
    low, high, far_up, far_down = lax.optimization_barrier((low, high, far_up, far_down))

    def spread(chosen):
        return moved(chosen, dz=1), moved(chosen, dz=3)

    def pass_on(back, ahead):
        return moved(back[:, :16], dz=1), moved(ahead[:, 16:], dz=3)

    def collect(chosen):
        back, ahead = spread(chosen)
        return jnp.concatenate([back, *pass_on(back, ahead), ahead], axis=1)

    def nothing(chosen):
        return jnp.zeros((chosen.shape[0], 96, WIDE), BF16)

    back, ahead = spread(low)
    low = (low, back, *pass_on(back, ahead), ahead)
    *low, high, wk_t, wv_t, wo_m = lax.optimization_barrier((*low, high, wk_t, wv_t, wo_m))
    high = (high, lax.cond(meta[0, 6] > FIRST, collect, nothing, high))
    *low, high, wo_m = lax.optimization_barrier((*low, high, wo_m))
    wo_t = [moved(w, dc=1) for w in wo_m]

    pieces = (*low, *high, *owns)
    w_parts = (w_out, *wo_m, *wo_t)
    wk, wv = (w_key, wk_m, wk_t), (w_value, wv_m, wv_t)
    heard = attend(0, sc, meta, (far_up, far_down), pieces, wk, wv)
    left, right = project(0, heard, w_parts)
    left, right, q_up = lax.optimization_barrier((left, right, q_up))
    above, below = moved(left, dz=1), moved(right, dz=3)
    heard = attend(1, sc, meta, (q_down, q_up), pieces, wk, wv)
    heard, above, below = lax.optimization_barrier((heard, above, below))
    up, down = project(1, heard, w_parts, (above, below))
    up, down, q_own = lax.optimization_barrier((up, down, q_own))
    up, down = moved(up, dz=1), moved(down, dz=3)
    heard = attend(2, sc, meta, (q_own,), pieces, wk, wv)
    heard, up, down = lax.optimization_barrier((heard, up, down))
    return project(2, heard, w_parts, (up, down))


def solution(mesh):
    in_specs = (
        P(("blk", "uly"), None),
        P(("blk", "uly"), None),
        P(),
        P(None, "uly"),
        P(None, "uly"),
        P("uly", None),
    )
    out_specs = P(("blk", "uly"), None)
    return jax.shard_map(local, mesh=mesh, in_specs=in_specs, out_specs=out_specs, check_vma=False)
```
